256 devices in a mesh: seq: 32 (over y, z), mp: 8 (over x, core).
Axes of the slice: x: 4, y: 4, z: 8, core: 2. Of those that a mesh axis runs over, the one named last changes fastest.
Arguments:
- queries: bfloat16 [512, 8192], P('seq', 'mp'), may hold values from -64 to 64
- prefix_keys: bfloat16 [131072, 1024], P('seq', 'mp'), may hold values from -24 to 24
- prefix_values: bfloat16 [131072, 1024], P('seq', 'mp'), may hold values from -6 to 6
- resp_keys: bfloat16 [512, 1024], P('seq', 'mp'), may hold values from -28 to 28
- resp_values: bfloat16 [512, 1024], P('seq', 'mp'), may hold values from -6 to 6
- segment_ids: int32 [512], replicated, may hold values from 0 to 3, never falling along the last dimension, each value on 1 to 256 neighbouring positions
- out_weight: bfloat16 [8192, 8192], P('mp', 'seq'), may hold values from -0.0625 to 0.0625
Outputs:
- scored: bfloat16 [512, 8192], P('mp', 'seq')
The draws below stay inside these ranges and needn't reach their ends.
Inputs may be any that keep to these rules, and one draw needn't show every extreme that they name: `segment_ids`: never falling; each of the 4 responses holds 1 to 256 tokens, one exactly 256.
All inputs are finite; a program needn't handle non-finite values.
Results may differ from the reference program's by a relative error of at most 0.013.
Values may be sent and summed in bfloat16 or wider, within the bound.
No kernel may reach another device: no remote copies, remote signals or barrier semaphores. Data moves between devices by JAX's collectives and lax.ppermute only.
A program may use at most 64 MiB of HBM per device.

```python
import math
import jax
import jax.numpy as jnp
import numpy as np
from jax import lax

D = 8192
HQ = 64
KVH = 8
HD = 128
RESP = 512
PREFIX = 131072


def draw_queries(key, part):
    key = jax.random.fold_in(key, 11)
    base = jnp.clip(jax.random.normal(key, (RESP, HQ * HD), jnp.float32), -6.0, 6.0)
    return base.astype(jnp.bfloat16)


def draw_prefix_keys(key, part):
    key = jax.random.fold_in(key, 12)
    base = 1.5 * jnp.clip(jax.random.normal(key, (PREFIX, KVH * HD), jnp.float32), -8.0, 8.0)
    return base.astype(jnp.bfloat16)


def levels(own_key, shape, pieces, low, largest):
    def one(axis_at, shards_of):
        heights = jax.random.uniform(jax.random.fold_in(jax.random.fold_in(own_key, 6), axis_at), (shards_of,), jnp.float32, low / len(pieces), largest / len(pieces))
        return jnp.repeat(jnp.exp(heights), shape[axis_at] // shards_of).reshape((-1,) + (1,) * (len(shape) - axis_at - 1))

    factor_of = one(*pieces[0])
    for cut in pieces[1:]:
        factor_of = factor_of * one(*cut)
    return factor_of


def length_profile(number_of, total, bound, lean):
    portions = [(1 << 20) // math.isqrt(rank ** lean) + 1 for rank in range(2, number_of + 1)]
    spare, holding = total - bound - (number_of - 1), [1] * (number_of - 1)
    while spare > 0:
        movable = [i for i in range(number_of - 1) if holding[i] < bound]
        whole, budget = sum([portions[i] for i in movable]), spare
        for i in movable:
            extra = min(bound - holding[i], max(1, budget * portions[i] // whole), spare)
            holding[i] = holding[i] + extra
            spare = spare - extra
    return np.array([bound] + holding)


def ragged(rng, number_of, total, reach, slope):
    if number_of == 2:
        one = jax.random.randint(rng, (), max(1, total - reach), min(reach, total - 1) + 1)
        return jnp.stack([one, total - one])
    tallies = jnp.asarray(length_profile(number_of, total, reach, slope), jnp.int32)
    twos = (number_of - 1) // 2
    donor, sink = tallies[1:1 + 2 * twos:2], tallies[2:2 + 2 * twos:2]
    slack = jnp.minimum(donor - 1, reach - sink)
    shifted = jax.random.randint(jax.random.fold_in(rng, 1), (twos,), 0, 1 << 20) % (slack + 1)
    tallies = tallies.at[1:1 + 2 * twos:2].set(donor - shifted).at[2:2 + 2 * twos:2].set(sink + shifted)
    return tallies[jax.random.permutation(jax.random.fold_in(rng, 2), number_of)]


def bell_draw(rng, dims, spread, most, pieces=(), kind=jnp.bfloat16):
    values = spread * jax.random.normal(rng, dims, jnp.float32)
    if pieces:
        values = values * levels(rng, dims, pieces, -0.22, 0.18)
    return jnp.clip(values, -most, most).astype(kind)


def setup_inputs(seed: int = 0) -> dict:
    key_list = jax.random.split(jax.random.key(seed), 8)
    return {
        "queries": draw_queries(jax.random.fold_in(key_list[7], 71), 0),
        "prefix_keys": draw_prefix_keys(jax.random.fold_in(key_list[7], 71), 0),
        "prefix_values": bell_draw(key_list[2], (PREFIX, KVH * HD), 1.0, 6.0, ((0, 32), (1, 8))),
        "resp_keys": bell_draw(key_list[3], (RESP, KVH * HD), 3.5, 28.0, ((0, 32), (1, 8))),
        "resp_values": bell_draw(key_list[4], (RESP, KVH * HD), 1.0, 6.0, ((0, 32), (1, 8))),
        "segment_ids": jnp.searchsorted(jnp.cumsum(ragged(key_list[5], 4, RESP, RESP // 2, 2)), jnp.arange(RESP), side="right").astype(jnp.int32),
        "out_weight": bell_draw(key_list[6], (HQ * HD, D), (HQ * HD) ** -0.5, 0.0625, ((0, 8), (1, 32))),
    }


def reference(queries, prefix_keys, prefix_values, resp_keys, resp_values, segment_ids, out_weight):
    group = HQ // KVH
    width = RESP * group
    block = min(512, PREFIX)
    blocks = PREFIX // block
    scale = HD ** -0.5
    query_heads = queries.reshape(RESP, KVH, group, HD).transpose(1, 0, 2, 3).reshape(KVH, width, HD)
    keys_heads = prefix_keys.reshape(PREFIX, KVH, HD).transpose(1, 0, 2)
    values_heads = prefix_values.reshape(PREFIX, KVH, HD).transpose(1, 0, 2)
    own_keys = resp_keys.reshape(RESP, KVH, HD).transpose(1, 0, 2)
    own_values = resp_values.reshape(RESP, KVH, HD).transpose(1, 0, 2)
    row_token = jnp.arange(width, dtype=jnp.int32) // group
    columns = jnp.arange(RESP, dtype=jnp.int32)
    allowed = (segment_ids[row_token][:, None] == segment_ids[None, :]) & (columns[None, :] <= row_token[:, None])

    def update(state, scores, values):
        peak, total, weighted = state
        new_peak = jnp.maximum(peak, jnp.max(scores, axis=1))
        factor = jnp.exp(peak - new_peak)
        weights = jnp.exp(scores - new_peak[:, None])
        total = total * factor + jnp.sum(weights, axis=1)
        weighted = weighted * factor[:, None] + jnp.dot(weights.astype(jnp.bfloat16), values, preferred_element_type=jnp.float32)
        return (new_peak, total, weighted)

    def one_head(head):
        query_rows = query_heads[head]
        keys_all = keys_heads[head]
        values_all = values_heads[head]

        def step(state, index):
            start = (index * block).astype(jnp.int32)
            key_block = lax.dynamic_slice_in_dim(keys_all, start, block, 0)
            value_block = lax.dynamic_slice_in_dim(values_all, start, block, 0)
            scores = jnp.dot(query_rows, key_block.T, preferred_element_type=jnp.float32) * scale
            return update(state, scores, value_block), None

        start_state = (jnp.full((width,), -1e30, jnp.float32), jnp.zeros((width,), jnp.float32), jnp.zeros((width, HD), jnp.float32))
        state, _ = lax.scan(step, start_state, jnp.arange(blocks, dtype=jnp.int32))
        scores = jnp.dot(query_rows, own_keys[head].T, preferred_element_type=jnp.float32) * scale
        scores = jnp.where(allowed, scores, jnp.float32(-1e30))
        peak, total, weighted = update(state, scores, own_values[head])
        return (weighted / total[:, None]).astype(jnp.bfloat16)

    heads = lax.map(one_head, jnp.arange(KVH, dtype=jnp.int32))
    attended = heads.reshape(KVH, RESP, group, HD).transpose(1, 0, 2, 3).reshape(RESP, HQ * HD)
    return jnp.dot(attended, out_weight, preferred_element_type=jnp.float32).astype(jnp.bfloat16)
```

```python
import jax
import jax.numpy as jnp
from jax import lax
from jax.experimental import pallas as pl
from jax.experimental.pallas import tpu as pltpu
from jax.sharding import PartitionSpec as P

HD = 128
SCALE2 = HD**-0.5 * 1.4426950408889634
LIMIT = 64.0
SMALL = 2.0**-20
f32 = jnp.float32
bf16 = jnp.bfloat16


def attend_kernel(
    group, key_block, q_ref, k_ref, v_ref, rk_ref, rv_ref, bias_ref, out_ref,
    kt_ref, ve_ref, s_ref, logs_ref, facts_ref,
):
    head = pl.program_id(0)
    keys = k_ref.shape[0]
    rows = q_ref.shape[0]
    owners = out_ref.shape[0]
    own = rk_ref.shape[0]

    @pl.when(head == 0)
    def _():
        kt = k_ref[...].T
        kt_ref[:, :keys] = kt
        kt_ref[:, keys:] = jnp.zeros((HD, HD), bf16)
        kt_ref[:, keys : keys + HD] = jnp.concatenate(
            [rk_ref[...], jnp.zeros((HD - own, HD), bf16)], axis=0
        ).T
        ve_ref[:keys, :HD] = v_ref[...]
        ve_ref[keys:, :HD] = jnp.concatenate(
            [rv_ref[...], jnp.zeros((HD - own, HD), bf16)], axis=0
        )
        ve_ref[:, HD:] = jnp.ones((keys + HD, HD), bf16)
        logs_ref[...] = jnp.zeros_like(logs_ref)
        square = kt.astype(f32)
        facts_ref[0] = jnp.max(jnp.sum(square * square, axis=0, keepdims=True))
        facts_ref[1] = jnp.max(jnp.abs(v_ref[...].astype(f32)))

    @pl.when(head < group)
    def _():
        q = q_ref[...]

        def scores(start, size):
            return jnp.dot(q, kt_ref[:, start : start + size], preferred_element_type=f32)

        def own_scores():
            return scores(keys, HD) * SCALE2 + bias_ref[...]

        def product(weights, start, size):
            return jnp.dot(
                weights.astype(bf16), ve_ref[start : start + size, :], preferred_element_type=f32
            )

        def finish(total, shift):
            denominator = total[:, HD:]
            result = total[:, :HD] / denominator
            out_ref[...] = result.astype(bf16).reshape(owners, rows // owners, HD)
            log = jnp.log2(denominator) + shift
            high = log.astype(bf16).astype(f32)
            rest = log - high
            middle = rest.astype(bf16).astype(f32)
            low = (rest - middle).astype(bf16).astype(f32)
            lane = lax.broadcasted_iota(jnp.int32, (rows, HD), 1)
            logs_ref[...] += jnp.where(
                lane == head,
                high,
                jnp.where(
                    lane == head + group, middle, jnp.where(lane == head + 2 * group, low, 0.0)
                ),
            )

        qf = q.astype(f32)
        longest = jnp.max(jnp.sum(qf * qf, axis=1, keepdims=True))
        inside = (
            (longest * facts_ref[0] * (SCALE2 * SCALE2) <= LIMIT * LIMIT)
            & (jnp.max(own_scores()) <= LIMIT)
            & (facts_ref[1] >= SMALL)
        )

        @pl.when(inside)
        def _():
            total = product(jnp.exp2(own_scores()), keys, HD)
            now = scores(0, key_block)
            for start in range(0, keys, key_block):
                later = start + key_block
                if later < keys:
                    following = scores(later, key_block)
                total += product(jnp.exp2(now * SCALE2), start, key_block)
                if later < keys:
                    now = following
            finish(total, 0.0)

        @pl.when(jnp.logical_not(inside))
        def _():
            mine = own_scores()
            top = mine
            for start in range(0, keys, key_block):
                part = scores(start, key_block) * SCALE2
                s_ref[:, start : start + key_block] = part
                for lanes in range(0, key_block, HD):
                    top = jnp.maximum(top, part[:, lanes : lanes + HD])
            top = jnp.max(top, axis=1, keepdims=True)
            total = product(jnp.exp2(mine - top), keys, HD)
            for start in range(0, keys, key_block):
                part = s_ref[:, start : start + key_block]
                total += product(jnp.exp2(part - top), start, key_block)
            finish(total, top)

    @pl.when(head == group)
    def _():
        out_ref[...] = logs_ref[...].astype(bf16).reshape(owners, rows // owners, HD)


def attend(queries, keys, values, own_keys, own_values, bias, owners):
    rows, width = queries.shape
    group = width // HD
    count = keys.shape[0]
    tokens = rows // owners
    whole = lambda array: pl.BlockSpec(array.shape, lambda head: (0, 0))
    return pl.pallas_call(
        lambda *refs: attend_kernel(group, 256, *refs),
        grid=(group + 1,),
        out_shape=jax.ShapeDtypeStruct((owners, (group + 1) * tokens, HD), bf16),
        in_specs=[
            pl.BlockSpec((rows, HD), lambda head: (0, jnp.minimum(head, group - 1))),
            whole(keys),
            whole(values),
            whole(own_keys),
            whole(own_values),
            whole(bias),
        ],
        out_specs=pl.BlockSpec((owners, tokens, HD), lambda head: (0, head, 0)),
        scratch_shapes=[
            pltpu.VMEM((HD, count + HD), bf16),
            pltpu.VMEM((count + HD, 2 * HD), bf16),
            pltpu.VMEM((rows, count), f32),
            pltpu.VMEM((rows, HD), f32),
            pltpu.SMEM((2,), f32),
        ],
        compiler_params=pltpu.CompilerParams(vmem_limit_bytes=48 << 20),
        name="attend",
    )(queries, keys, values, own_keys, own_values, bias)


def combine_kernel(group, parts_ref, out_ref):
    owners, _, _ = parts_ref.shape
    copies, tokens, _ = out_ref.shape
    pieces = parts_ref[:, group * tokens :, :].astype(f32)
    logs = sum(pieces[:, :, piece * group : (piece + 1) * group] for piece in range(3))
    share = jnp.exp2(logs - jnp.max(logs, axis=0, keepdims=True))
    share = share / jnp.sum(share, axis=0, keepdims=True)
    for head in range(group):
        part = parts_ref[:, head * tokens : (head + 1) * tokens, :].astype(f32)
        result = jnp.sum(part * share[:, :, head : head + 1], axis=0).astype(bf16)
        out_ref[:, :, head * HD : (head + 1) * HD] = jnp.broadcast_to(
            result[None], (copies, tokens, HD)
        )


def combine(parts, copies):
    owners, height, _ = parts.shape
    tokens = 16 * (height // 144)
    group = height // tokens - 1
    return pl.pallas_call(
        lambda *refs: combine_kernel(group, *refs),
        out_shape=jax.ShapeDtypeStruct((copies, tokens, group * HD), bf16),
        compiler_params=pltpu.CompilerParams(vmem_limit_bytes=32 << 20),
        name="combine",
    )(parts)


def on_device(queries, prefix_keys, prefix_values, resp_keys, resp_values, segment_ids, out_weight):
    shards = lax.axis_size("seq")
    ways = lax.axis_size("mp")
    tokens = queries.shape[0]
    rows = segment_ids.shape[0]
    first = lax.axis_index("seq") * tokens
    own_segments = jnp.pad(lax.dynamic_slice_in_dim(segment_ids, first, tokens), (0, HD - tokens))
    column = jnp.arange(HD, dtype=jnp.int32)[None, :]
    allowed = (
        (column < tokens)
        & (segment_ids[:, None] == own_segments[None, :])
        & (first + column <= jnp.arange(rows, dtype=jnp.int32)[:, None])
    )
    bias = jnp.where(allowed, f32(0), f32(-1e30))

    copies = jnp.broadcast_to(queries[None], (shards,) + queries.shape)
    all_queries = lax.all_to_all(copies, "seq", 0, 0, tiled=True).reshape(rows, -1)
    parts = attend(
        all_queries, prefix_keys, prefix_values, resp_keys, resp_values, bias, shards
    )
    parts = lax.all_to_all(parts, "seq", 0, 0, tiled=True)
    heads = combine(parts, shards)
    heads = lax.all_to_all(heads, "seq", 0, 0, tiled=True).reshape(rows, -1)
    scored = jnp.dot(heads, out_weight, preferred_element_type=f32).astype(bf16)
    scored = scored.reshape(ways, rows // ways, -1)
    scored = lax.all_to_all(scored, "mp", 0, 0, tiled=True)
    return jnp.sum(scored.astype(f32), axis=0).astype(bf16)


def solution(mesh):
    in_specs = (
        P("seq", "mp"),
        P("seq", "mp"),
        P("seq", "mp"),
        P("seq", "mp"),
        P("seq", "mp"),
        P(),
        P("mp", "seq"),
    )
    return jax.shard_map(
        on_device, mesh=mesh, in_specs=in_specs, out_specs=P("mp", "seq"), check_vma=False
    )
```

```python
import jax
import jax.numpy as jnp
from jax import lax
from jax.experimental import pallas as pl
from jax.experimental.pallas import tpu as pltpu
from jax.sharding import PartitionSpec as P

HD = 128
SCALE2 = HD**-0.5 * 1.4426950408889634
LOWEST = 2.0**-60
HIGHEST = 2.0**100
SMALL = 2.0**-20
ONES = 16
DEPTH = 4
f32 = jnp.float32
bf16 = jnp.bfloat16


def split3(x):
    high = x.astype(bf16).astype(f32)
    rest = x - high
    middle = rest.astype(bf16).astype(f32)
    return high, middle, rest - middle


def prepare_kernel(v_ref, rv_ref, vt_ref, rvt_ref, fact_ref):
    v = v_ref[...]
    vt_ref[:HD, :] = v.T
    vt_ref[HD:, :] = jnp.ones((ONES, v.shape[0]), bf16)
    rvt_ref[:HD, :] = rv_ref[...].T
    rvt_ref[HD:, :] = jnp.ones((ONES, rv_ref.shape[0]), bf16)
    fact_ref[0, 0] = jnp.maximum(
        jnp.max(jnp.abs(v.astype(f32))), jnp.max(jnp.abs(rv_ref[...].astype(f32)))
    )


def prepare(values, own_values):
    vmem = pl.BlockSpec(memory_space=pltpu.VMEM)
    return pl.pallas_call(
        prepare_kernel,
        out_shape=(
            jax.ShapeDtypeStruct((HD + ONES, values.shape[0]), bf16),
            jax.ShapeDtypeStruct((HD + ONES, own_values.shape[0]), bf16),
            jax.ShapeDtypeStruct((1, 1), f32),
        ),
        out_specs=(vmem, vmem, pl.BlockSpec(memory_space=pltpu.SMEM)),
        name="prepare",
    )(values, own_values)


def attend_kernel(
    group, stack, key_block, q_ref, k_ref, vt_ref, rk_ref, rvt_ref, bias_ref, fact_ref, out_ref
):
    tokens = q_ref.shape[0]
    keys = k_ref.shape[0]

    def scores(keys_block, q):
        return (
            lax.dot_general(
                keys_block, q, (((1,), (1,)), ((), ())), preferred_element_type=f32
            )
            * SCALE2
        )

    def product(columns, weights):
        return jnp.dot(columns, weights.astype(bf16), preferred_element_type=f32)

    def result_of(total):
        return (total[:HD] / total[HD : HD + 1]).T.astype(bf16)

    def logs_rows(rows):
        pieces = split3(jnp.concatenate(rows, axis=0))
        out_ref[group * tokens :, :] = jnp.concatenate(
            pieces + (jnp.zeros((group, tokens), f32),), axis=0
        ).astype(bf16)

    lowest, highest = [], []
    logs = []
    bias = jnp.concatenate([bias_ref[...]] * stack, axis=1)
    for first in range(0, group, stack):
        q = jnp.concatenate(
            [q_ref[:, head * HD : (head + 1) * HD] for head in range(first, first + stack)], axis=0
        )
        total = product(rvt_ref[...], jnp.exp2(scores(rk_ref[...], q) + bias))
        now = scores(k_ref[:key_block, :], q)
        for start in range(0, keys, key_block):
            later = start + key_block
            if later < keys:
                following = scores(k_ref[later : later + key_block, :], q)
            total += product(vt_ref[:, start:later], jnp.exp2(now))
            if later < keys:
                now = following
        sums = total[HD : HD + 1]
        lowest.append(jnp.min(sums))
        highest.append(jnp.max(sums))
        log = jnp.log2(sums)
        for at in range(stack):
            lanes = slice(at * tokens, (at + 1) * tokens)
            logs.append(log[:, lanes])
            head = first + at
            out_ref[head * tokens : (head + 1) * tokens, :] = result_of(total[:, lanes])
    logs_rows(logs)
    inside = fact_ref[0, 0] >= SMALL
    for low, high in zip(lowest, highest):
        inside = inside & (low >= LOWEST) & (high <= HIGHEST)

    @pl.when(jnp.logical_not(inside))
    def _():
        logs = []
        for head in range(group):
            q = q_ref[:, head * HD : (head + 1) * HD]
            mine = scores(rk_ref[...], q) + bias_ref[...]
            rest = scores(k_ref[...], q)
            top = jnp.maximum(
                jnp.max(mine, axis=0, keepdims=True), jnp.max(rest, axis=0, keepdims=True)
            )
            total = product(rvt_ref[...], jnp.exp2(mine - top))
            total += product(vt_ref[...], jnp.exp2(rest - top))
            logs.append(jnp.log2(total[HD : HD + 1]) + top)
            out_ref[head * tokens : (head + 1) * tokens, :] = result_of(total)
        logs_rows(logs)


def attend(queries, keys, columns, own_keys, own_columns, bias, fact):
    tokens, width = queries.shape
    group = width // HD
    vmem = pl.BlockSpec(memory_space=pltpu.VMEM)
    return pl.pallas_call(
        lambda *refs: attend_kernel(group, min(4, group), 512, *refs),
        out_shape=jax.ShapeDtypeStruct((group * (tokens + DEPTH), HD), bf16),
        in_specs=[vmem] * 6 + [pl.BlockSpec(memory_space=pltpu.SMEM)],
        out_specs=vmem,
        compiler_params=pltpu.CompilerParams(vmem_limit_bytes=48 << 20),
        name="attend",
    )(queries, keys, columns, own_keys, own_columns, bias, fact)


def join_kernel(group, *refs):
    part_refs, out_ref = refs[:-1], refs[-1]
    owners = out_ref.shape[0]
    tokens = part_refs[0].shape[0] // group - DEPTH
    base = group * tokens
    logs = []
    for ref in part_refs:
        pieces = ref[base:, :].astype(f32)
        logs.append(sum(pieces[at * group : (at + 1) * group] for at in range(3)))
    top = logs[0]
    for log in logs[1:]:
        top = jnp.maximum(top, log)
    shares = [jnp.exp2(log - top) for log in logs]
    whole = sum(shares)
    shares = [share / whole for share in shares]
    rows = list(split3(top + jnp.log2(whole))) + shares
    rows.append(jnp.zeros((HD - group * len(rows), tokens), f32))
    turned = jnp.concatenate(rows, axis=0).T
    for head in range(group):
        total = None
        for at, ref in enumerate(part_refs):
            lane = (3 + at) * group + head
            term = ref[head * tokens : (head + 1) * tokens, :].astype(f32) * turned[
                :, lane : lane + 1
            ]
            total = term if total is None else total + term
        split = tokens // owners
        out_ref[:, head * split : (head + 1) * split, :] = total.astype(bf16).reshape(
            owners, split, HD
        )
    out_ref[:, group * split :, :] = turned.astype(bf16).reshape(owners, split, HD)


def join(parts, group, owners):
    tokens = parts[0].shape[0] // group - DEPTH
    return pl.pallas_call(
        lambda *refs: join_kernel(group, *refs),
        out_shape=jax.ShapeDtypeStruct((owners, (group + 1) * (tokens // owners), HD), bf16),
        compiler_params=pltpu.CompilerParams(vmem_limit_bytes=32 << 20),
        name="join",
    )(*parts)


def combine_kernel(group, parts_ref, out_ref):
    copies, tokens, _ = out_ref.shape
    pieces = parts_ref[:, group * tokens :, :].astype(f32)
    logs = sum(pieces[:, :, piece * group : (piece + 1) * group] for piece in range(3))
    share = jnp.exp2(logs - jnp.max(logs, axis=0, keepdims=True))
    share = share / jnp.sum(share, axis=0, keepdims=True)
    for head in range(group):
        part = parts_ref[:, head * tokens : (head + 1) * tokens, :].astype(f32)
        result = jnp.sum(part * share[:, :, head : head + 1], axis=0).astype(bf16)
        out_ref[:, :, head * HD : (head + 1) * HD] = jnp.broadcast_to(
            result[None], (copies, tokens, HD)
        )


def combine(parts, group):
    owners, height, _ = parts.shape
    return pl.pallas_call(
        lambda *refs: combine_kernel(group, *refs),
        out_shape=jax.ShapeDtypeStruct((owners, height // (group + 1), group * HD), bf16),
        compiler_params=pltpu.CompilerParams(vmem_limit_bytes=32 << 20),
        name="combine",
    )(parts)


Y, Z = 4, 8


def on_device(queries, prefix_keys, prefix_values, resp_keys, resp_values, segment_ids, out_weight):
    ways = lax.axis_size("mp")
    tokens, width = queries.shape
    group = width // HD
    rows = segment_ids.shape[0]
    quarter = rows // Y
    along_z = [[y * Z + z for z in range(Z)] for y in range(Y)]
    place = lax.axis_index("seq")

    def across_z(array):
        return lax.all_to_all(array, "seq", 0, 0, axis_index_groups=along_z, tiled=True)

    def along_y(array, step):
        pairs = [(y * Z + z, (y + step) % Y * Z + z) for y in range(Y) for z in range(Z)]
        return lax.ppermute(array, "seq", pairs)

    mine = across_z(jnp.broadcast_to(queries[None], (Z,) + queries.shape)).reshape(quarter, width)

    columns, own_columns, fact = prepare(prefix_values, resp_values)
    first = place * tokens
    own_segments = lax.dynamic_slice_in_dim(segment_ids, first, tokens)
    own_rows = first + jnp.arange(tokens, dtype=jnp.int32)
    allowed = (own_segments[:, None] == segment_ids[None, :]) & (
        own_rows[:, None] <= jnp.arange(rows, dtype=jnp.int32)[None, :]
    )
    bias = jnp.where(allowed, f32(0), f32(-1e30))

    def part_for(array, step):
        owner = (place // Z + Y - step) % Y
        block = lax.dynamic_slice_in_dim(bias, owner * quarter, quarter, 1)
        return attend(array, prefix_keys, columns, resp_keys, own_columns, block, fact)

    arrivals = {step: along_y(mine, step) for step in (1, 3, 2)}
    parts = [part_for(mine, 0)]
    for step in (1, 2, 3):
        parts.append(along_y(part_for(arrivals[step], step), -step))

    joined = across_z(join(parts, group, Z))
    heads = across_z(combine(joined, group)).reshape(quarter, width)
    pieces = [heads] + [along_y(heads, step) for step in (1, 3, 2)]
    scored = [
        jnp.dot(piece, out_weight, preferred_element_type=f32).astype(bf16) for piece in pieces
    ]
    order = (0, 1, 3, 2)
    whole = jnp.zeros((rows, out_weight.shape[1]), bf16)
    for step, piece in zip(order, scored):
        owner = (place // Z + Y - step) % Y
        whole = lax.dynamic_update_slice_in_dim(whole, piece, owner * quarter, 0)
    scored = whole.reshape(ways, rows // ways, -1)
    scored = lax.all_to_all(scored, "mp", 0, 0, tiled=True)
    return jnp.sum(scored.astype(f32), axis=0).astype(bf16)


def solution(mesh):
    in_specs = (
        P("seq", "mp"),
        P("seq", "mp"),
        P("seq", "mp"),
        P("seq", "mp"),
        P("seq", "mp"),
        P(),
        P("mp", "seq"),
    )
    return jax.shard_map(
        on_device, mesh=mesh, in_specs=in_specs, out_specs=P("mp", "seq"), check_vma=False
    )
```

```python
import jax
import jax.numpy as jnp
from jax import lax
from jax.experimental import pallas as pl
from jax.experimental.pallas import tpu as pltpu
from jax.sharding import PartitionSpec as P

HD = 128
SCALE2 = HD**-0.5 * 1.4426950408889634
LOWEST = 2.0**-60
HIGHEST = 2.0**100
SMALL = 2.0**-20
ONES = 16
f32 = jnp.float32
bf16 = jnp.bfloat16


def split3(x):
    high = x.astype(bf16).astype(f32)
    rest = x - high
    middle = rest.astype(bf16).astype(f32)
    return high, middle, rest - middle


def prepare_kernel(v_ref, rv_ref, vt_ref, rvt_ref, fact_ref):
    v = v_ref[...]
    vt_ref[:HD, :] = v.T
    vt_ref[HD:, :] = jnp.ones((ONES, v.shape[0]), bf16)
    rvt_ref[:HD, :] = rv_ref[...].T
    rvt_ref[HD:, :] = jnp.ones((ONES, rv_ref.shape[0]), bf16)
    fact_ref[0, 0] = jnp.maximum(
        jnp.max(jnp.abs(v.astype(f32))), jnp.max(jnp.abs(rv_ref[...].astype(f32)))
    )


def prepare(values, own_values):
    vmem = pl.BlockSpec(memory_space=pltpu.VMEM)
    return pl.pallas_call(
        prepare_kernel,
        out_shape=(
            jax.ShapeDtypeStruct((HD + ONES, values.shape[0]), bf16),
            jax.ShapeDtypeStruct((HD + ONES, own_values.shape[0]), bf16),
            jax.ShapeDtypeStruct((1, 1), f32),
        ),
        out_specs=(vmem, vmem, pl.BlockSpec(memory_space=pltpu.SMEM)),
        name="prepare",
    )(values, own_values)


def attend_tile(q_of, bias, put, group, k_ref, vt_ref, rk_ref, rvt_ref, fact_ref):
    keys = k_ref.shape[0]
    tile = bias.shape[1]
    stack = min(STACK, group)

    def scores(keys_block, q):
        return (
            lax.dot_general(
                keys_block, q, (((1,), (1,)), ((), ())), preferred_element_type=f32
            )
            * SCALE2
        )

    def product(columns, weights):
        return jnp.dot(columns, weights.astype(bf16), preferred_element_type=f32)

    def put_result(head, total):
        put(head, (total[:HD] / total[HD : HD + 1]).T.astype(bf16))

    def put_logs(logs):
        pieces = split3(jnp.concatenate(logs, axis=0))
        pieces += (jnp.zeros((HD - len(pieces) * group, tile), f32),)
        put(group, jnp.concatenate(pieces, axis=0).T.astype(bf16))

    inside = fact_ref[0, 0] >= SMALL
    logs = []
    wide_bias = jnp.concatenate([bias] * stack, axis=1)
    for first in range(0, group, stack):
        q = jnp.concatenate([q_of(head) for head in range(first, first + stack)], axis=0)
        total = product(rvt_ref[...], jnp.exp2(scores(rk_ref[...], q) + wide_bias))
        now = scores(k_ref[:KEY_BLOCK, :], q)
        for start in range(0, keys, KEY_BLOCK):
            later = start + KEY_BLOCK
            if later < keys:
                following = scores(k_ref[later : later + KEY_BLOCK, :], q)
            total += product(vt_ref[:, start:later], jnp.exp2(now))
            if later < keys:
                now = following
        sums = total[HD : HD + 1]
        inside = inside & (jnp.min(sums) >= LOWEST) & (jnp.max(sums) <= HIGHEST)
        log = jnp.log2(sums)
        for at in range(stack):
            lanes = slice(at * tile, (at + 1) * tile)
            logs.append(log[:, lanes])
            put_result(first + at, total[:, lanes])
    put_logs(logs)

    @pl.when(jnp.logical_not(inside))
    def _():
        logs = []
        for head in range(group):
            q = q_of(head)
            mine = scores(rk_ref[...], q) + bias
            rest = scores(k_ref[...], q)
            top = jnp.maximum(
                jnp.max(mine, axis=0, keepdims=True), jnp.max(rest, axis=0, keepdims=True)
            )
            total = product(rvt_ref[...], jnp.exp2(mine - top))
            total += product(vt_ref[...], jnp.exp2(rest - top))
            logs.append(jnp.log2(total[HD : HD + 1]) + top)
            put_result(head, total)
        put_logs(logs)


def attend_own_kernel(at_ref, q_ref, bias_ref, k_ref, vt_ref, rk_ref, rvt_ref, fact_ref, out_ref):
    tile, width = q_ref.shape
    group = width // HD
    own = rk_ref.shape[0]

    def put(slot, value):
        out_ref[:, slot * own : (slot + 1) * own, :] = value.reshape(tile // own, own, HD)

    start = pl.multiple_of(at_ref[0] * tile, tile)
    attend_tile(
        lambda head: q_ref[:, head * HD : (head + 1) * HD],
        bias_ref[:, pl.ds(start, tile)],
        put, group, k_ref, vt_ref, rk_ref, rvt_ref, fact_ref,
    )


def attend_others_kernel(
    at_ref, q_ref, own_ref, bias_ref, k_ref, vt_ref, rk_ref, rvt_ref, fact_ref, out_ref
):
    sides, tile, width = q_ref.shape
    group = width // HD
    own = rk_ref.shape[0]
    blocks = tile // own
    me = at_ref[0]

    def put_block(side, block, slot, value):
        row = slot * tile + (side * (blocks // Y) + block // Y) * own
        out_ref[block % Y, pl.ds(pl.multiple_of(row, own), own), :] = value

    for block in range(blocks):
        for slot in range(group + 1):
            put_block(me, block, slot, own_ref[block, slot * own : (slot + 1) * own, :])

    @pl.loop(1, sides)
    def _(step):
        side = lax.rem(me + step, sides)

        def put(slot, value):
            for block in range(blocks):
                put_block(side, block, slot, value[block * own : (block + 1) * own])

        start = pl.multiple_of(side * tile, tile)
        attend_tile(
            lambda head: q_ref[side, :, head * HD : (head + 1) * HD],
            bias_ref[:, pl.ds(start, tile)],
            put, group, k_ref, vt_ref, rk_ref, rvt_ref, fact_ref,
        )


def in_vmem(kernel, name, out_shape, scalars, *arrays):
    smem = pl.BlockSpec(memory_space=pltpu.SMEM)
    vmem = pl.BlockSpec(memory_space=pltpu.VMEM)
    return pl.pallas_call(
        kernel,
        out_shape=jax.ShapeDtypeStruct(out_shape, bf16),
        in_specs=[smem if at in scalars else vmem for at in range(len(arrays))],
        out_specs=vmem,
        compiler_params=pltpu.CompilerParams(vmem_limit_bytes=20 << 20),
        name=name,
    )(*arrays)


def join_kernel(group, parts_ref, out_ref):
    owners = out_ref.shape[0]
    tile = parts_ref.shape[1] // (group + 1)
    own = tile // owners
    pieces = parts_ref[:, group * tile :, :].astype(f32)
    logs = sum(pieces[:, :, at * group : (at + 1) * group] for at in range(3))
    top = jnp.max(logs, axis=0)
    share = jnp.exp2(logs - top[None])
    whole = jnp.sum(share, axis=0)
    share = share / whole[None]
    for head in range(group):
        part = parts_ref[:, head * tile : (head + 1) * tile, :].astype(f32)
        total = jnp.sum(part * share[:, :, head : head + 1], axis=0)
        out_ref[:, head * own : (head + 1) * own, :] = total.astype(bf16).reshape(owners, own, HD)
    lanes = split3(top + jnp.log2(whole)) + (jnp.zeros((tile, HD - 3 * group), f32),)
    out_ref[:, group * own :, :] = (
        jnp.concatenate(lanes, axis=1).astype(bf16).reshape(owners, own, HD)
    )


def combine_kernel(group, parts_ref, out_ref):
    copies, tokens, _ = out_ref.shape
    pieces = parts_ref[:, group * tokens :, :].astype(f32)
    logs = sum(pieces[:, :, piece * group : (piece + 1) * group] for piece in range(3))
    share = jnp.exp2(logs - jnp.max(logs, axis=0, keepdims=True))
    share = share / jnp.sum(share, axis=0, keepdims=True)
    for head in range(group):
        part = parts_ref[:, head * tokens : (head + 1) * tokens, :].astype(f32)
        result = jnp.sum(part * share[:, :, head : head + 1], axis=0).astype(bf16)
        out_ref[:, :, head * HD : (head + 1) * HD] = jnp.broadcast_to(
            result[None], (copies, tokens, HD)
        )


def combine(parts, group):
    owners, height, _ = parts.shape
    return pl.pallas_call(
        lambda *refs: combine_kernel(group, *refs),
        out_shape=jax.ShapeDtypeStruct((owners, height // (group + 1), group * HD), bf16),
        compiler_params=pltpu.CompilerParams(vmem_limit_bytes=20 << 20),
        name="combine",
    )(parts)


def project_kernel(heads_ref, weight_ref, out_ref):
    heads = heads_ref[...]
    for at in range(weight_ref.shape[0]):
        out_ref[at] = jnp.dot(heads, weight_ref[at], preferred_element_type=f32).astype(bf16)


Y, Z = 4, 8
STACK = 4
KEY_BLOCK = 512


def on_device(queries, prefix_keys, prefix_values, resp_keys, resp_values, segment_ids, out_weight):
    ways = lax.axis_size("mp")
    tokens, width = queries.shape
    group = width // HD
    rows = segment_ids.shape[0]
    tile = rows // Y
    along_z = [[y * Z + z for z in range(Z)] for y in range(Y)]
    along_y = [[y * Z + z for y in range(Y)] for z in range(Z)]
    along_y_mp = [[s * ways + m for s in line for m in range(ways)] for line in along_y]
    place = lax.axis_index("seq")
    side = (place // Z).astype(jnp.int32).reshape(1)

    def exchange(array, groups, axis="seq"):
        return lax.all_to_all(array, axis, 0, 0, axis_index_groups=groups, tiled=True)

    def copies(array, count):
        return jnp.broadcast_to(array[None], (count,) + array.shape)

    weights = lax.all_gather(out_weight, "seq", axis=0, axis_index_groups=along_y)
    mine = exchange(copies(queries, Z), along_z).reshape(tile, width)

    columns, own_columns, fact = prepare(prefix_values, resp_values)
    first = place * tokens
    own_segments = lax.dynamic_slice_in_dim(segment_ids, first, tokens)
    own_rows = first + jnp.arange(tokens, dtype=jnp.int32)
    allowed = (own_segments[:, None] == segment_ids[None, :]) & (
        own_rows[:, None] <= jnp.arange(rows, dtype=jnp.int32)[None, :]
    )
    bias = jnp.where(allowed, f32(0), f32(-1e30))
    local = (bias, prefix_keys, columns, resp_keys, own_columns, fact)

    others = exchange(copies(mine, Y), along_y)
    own = in_vmem(
        attend_own_kernel, "attend_own", (Z, (group + 1) * tokens, HD), (0, 7), side, mine, *local
    )
    parts = in_vmem(
        attend_others_kernel, "attend_others", (Y, (group + 1) * tile, HD), (0, 8),
        side, others, own, *local,
    )
    parts = exchange(parts, along_y)
    parts = in_vmem(
        lambda *refs: join_kernel(group, *refs), "join", (Z, (group + 1) * tokens, HD), (), parts
    )
    heads = exchange(combine(exchange(parts, along_z), group), along_z).reshape(tile, width)
    scored = in_vmem(
        project_kernel, "project", (Y, tile, out_weight.shape[1]), (), heads, weights
    )
    scored = exchange(
        scored.reshape(Y * ways, tile // ways, -1), along_y_mp, ("seq", "mp")
    ).reshape(Y, ways, tile // ways, -1)
    return jnp.sum(scored.astype(f32), axis=1).astype(bf16).reshape(rows // ways, -1)


def solution(mesh):
    in_specs = (
        P("seq", "mp"),
        P("seq", "mp"),
        P("seq", "mp"),
        P("seq", "mp"),
        P("seq", "mp"),
        P(),
        P("mp", "seq"),
    )
    return jax.shard_map(
        on_device, mesh=mesh, in_specs=in_specs, out_specs=P("mp", "seq"), check_vma=False
    )
```

```python
import jax
import jax.numpy as jnp
from jax import lax
from jax.experimental import pallas as pl
from jax.experimental.pallas import tpu as pltpu
from jax.sharding import PartitionSpec as P

HD = 128
SCALE2 = HD**-0.5 * 1.4426950408889634
LOWEST = 2.0**-60
HIGHEST = 2.0**100
SMALL = 2.0**-20
ONES = 16
DEPTH = 4
f32 = jnp.float32
bf16 = jnp.bfloat16


def split3(x):
    high = x.astype(bf16).astype(f32)
    rest = x - high
    middle = rest.astype(bf16).astype(f32)
    return high, middle, rest - middle


def prepare_kernel(v_ref, rv_ref, vt_ref, rvt_ref, fact_ref):
    v = v_ref[...]
    vt_ref[:HD, :] = v.T
    vt_ref[HD:, :] = jnp.ones((ONES, v.shape[0]), bf16)
    rvt_ref[:HD, :] = rv_ref[...].T
    rvt_ref[HD:, :] = jnp.ones((ONES, rv_ref.shape[0]), bf16)
    fact_ref[0, 0] = jnp.maximum(
        jnp.max(jnp.abs(v.astype(f32))), jnp.max(jnp.abs(rv_ref[...].astype(f32)))
    )


def prepare(values, own_values):
    vmem = pl.BlockSpec(memory_space=pltpu.VMEM)
    return pl.pallas_call(
        prepare_kernel,
        out_shape=(
            jax.ShapeDtypeStruct((HD + ONES, values.shape[0]), bf16),
            jax.ShapeDtypeStruct((HD + ONES, own_values.shape[0]), bf16),
            jax.ShapeDtypeStruct((1, 1), f32),
        ),
        out_specs=(vmem, vmem, pl.BlockSpec(memory_space=pltpu.SMEM)),
        name="prepare",
    )(values, own_values)


def attend_kernel(
    group, stack, key_block, q_ref, k_ref, vt_ref, rk_ref, rvt_ref, bias_ref, fact_ref, out_ref,
    logs_ref,
):
    tokens = q_ref.shape[0]
    keys = k_ref.shape[0]

    def scores(keys_block, q):
        return (
            lax.dot_general(
                keys_block, q, (((1,), (1,)), ((), ())), preferred_element_type=f32
            )
            * SCALE2
        )

    def product(columns, weights):
        return jnp.dot(columns, weights.astype(bf16), preferred_element_type=f32)

    def result_of(total):
        return (total[:HD] / total[HD : HD + 1]).T.astype(bf16)

    def logs_rows(rows):
        pieces = split3(jnp.concatenate(rows, axis=0))
        out_ref[group * tokens :, :] = jnp.concatenate(
            pieces + (jnp.zeros((group, tokens), f32),), axis=0
        ).astype(bf16)

    lowest, highest = [], []
    logs = []
    bias = jnp.concatenate([bias_ref[...]] * stack, axis=1)
    for first in range(0, group, stack):
        q = jnp.concatenate(
            [q_ref[:, head * HD : (head + 1) * HD] for head in range(first, first + stack)], axis=0
        )
        total = product(rvt_ref[...], jnp.exp2(scores(rk_ref[...], q) + bias))
        now = scores(k_ref[:key_block, :], q)
        for start in range(0, keys, key_block):
            later = start + key_block
            if later < keys:
                following = scores(k_ref[later : later + key_block, :], q)
            total += product(vt_ref[:, start:later], jnp.exp2(now))
            if later < keys:
                now = following
        sums = total[HD : HD + 1]
        lowest.append(jnp.min(sums))
        highest.append(jnp.max(sums))
        log = jnp.log2(sums)
        for at in range(stack):
            lanes = slice(at * tokens, (at + 1) * tokens)
            logs.append(log[:, lanes])
            head = first + at
            out_ref[head * tokens : (head + 1) * tokens, :] = result_of(total[:, lanes])
    logs_rows(logs)
    inside = fact_ref[0, 0] >= SMALL
    for low, high in zip(lowest, highest):
        inside = inside & (low >= LOWEST) & (high <= HIGHEST)

    @pl.when(jnp.logical_not(inside))
    def _():
        @pl.loop(0, group)
        def _(head):
            q = q_ref[:, pl.ds(pl.multiple_of(head * HD, HD), HD)]
            mine = scores(rk_ref[...], q) + bias_ref[...]
            rest = scores(k_ref[...], q)
            top = jnp.maximum(
                jnp.max(mine, axis=0, keepdims=True), jnp.max(rest, axis=0, keepdims=True)
            )
            total = product(rvt_ref[...], jnp.exp2(mine - top))
            total += product(vt_ref[...], jnp.exp2(rest - top))
            logs_ref[pl.ds(head, 1), :] = jnp.log2(total[HD : HD + 1]) + top
            out_ref[pl.ds(pl.multiple_of(head * tokens, tokens), tokens), :] = result_of(total)

        logs_rows([logs_ref[...]])


def attend(queries, keys, columns, own_keys, own_columns, bias, fact):
    tokens, width = queries.shape
    group = width // HD
    vmem = pl.BlockSpec(memory_space=pltpu.VMEM)
    return pl.pallas_call(
        lambda *refs: attend_kernel(group, min(4, group), 512, *refs),
        out_shape=jax.ShapeDtypeStruct((group * (tokens + DEPTH), HD), bf16),
        in_specs=[vmem] * 6 + [pl.BlockSpec(memory_space=pltpu.SMEM)],
        out_specs=vmem,
        scratch_shapes=[pltpu.VMEM((group, tokens), f32)],
        compiler_params=pltpu.CompilerParams(vmem_limit_bytes=20 << 20),
        name="attend",
    )(queries, keys, columns, own_keys, own_columns, bias, fact)


def join_kernel(group, halves, *refs):
    own_refs, part_refs, out_ref = refs[:halves], refs[halves:-1], refs[-1]
    owners = out_ref.shape[0]
    tokens = part_refs[0].shape[0] // group - DEPTH
    few = group // halves

    def log_of(ref, heads):
        pieces = ref[heads * tokens :, :].astype(f32)
        return sum(pieces[at * heads : (at + 1) * heads] for at in range(3))

    def part_of(at, head):
        ref = part_refs[at - 1] if at else own_refs[head // few]
        row = head * tokens if at else head % few * tokens
        return ref[row : row + tokens, :].astype(f32)

    logs = [jnp.concatenate([log_of(ref, few) for ref in own_refs], axis=0)]
    logs += [log_of(ref, group) for ref in part_refs]
    top = logs[0]
    for log in logs[1:]:
        top = jnp.maximum(top, log)
    shares = [jnp.exp2(log - top) for log in logs]
    whole = sum(shares)
    shares = [share / whole for share in shares]
    rows = list(split3(top + jnp.log2(whole))) + shares
    rows.append(jnp.zeros((HD - group * len(rows), tokens), f32))
    turned = jnp.concatenate(rows, axis=0).T
    split = tokens // owners
    for head in range(group):
        total = None
        for at in range(len(shares)):
            lane = (3 + at) * group + head
            term = part_of(at, head) * turned[:, lane : lane + 1]
            total = term if total is None else total + term
        out_ref[:, head * split : (head + 1) * split, :] = total.astype(bf16).reshape(
            owners, split, HD
        )
    out_ref[:, group * split :, :] = turned.astype(bf16).reshape(owners, split, HD)


def join(own, parts, group, owners):
    tokens = parts[0].shape[0] // group - DEPTH
    return pl.pallas_call(
        lambda *refs: join_kernel(group, len(own), *refs),
        out_shape=jax.ShapeDtypeStruct((owners, (group + 1) * (tokens // owners), HD), bf16),
        compiler_params=pltpu.CompilerParams(vmem_limit_bytes=20 << 20),
        name="join",
    )(*own, *parts)


def combine_kernel(group, parts_ref, out_ref):
    copies, tokens, _ = out_ref.shape
    pieces = parts_ref[:, group * tokens :, :].astype(f32)
    logs = sum(pieces[:, :, piece * group : (piece + 1) * group] for piece in range(3))
    share = jnp.exp2(logs - jnp.max(logs, axis=0, keepdims=True))
    share = share / jnp.sum(share, axis=0, keepdims=True)
    for head in range(group):
        part = parts_ref[:, head * tokens : (head + 1) * tokens, :].astype(f32)
        result = jnp.sum(part * share[:, :, head : head + 1], axis=0).astype(bf16)
        out_ref[:, :, head * HD : (head + 1) * HD] = jnp.broadcast_to(
            result[None], (copies, tokens, HD)
        )


def combine(parts, group):
    owners, height, _ = parts.shape
    return pl.pallas_call(
        lambda *refs: combine_kernel(group, *refs),
        out_shape=jax.ShapeDtypeStruct((owners, height // (group + 1), group * HD), bf16),
        compiler_params=pltpu.CompilerParams(vmem_limit_bytes=20 << 20),
        name="combine",
    )(parts)


Y, Z = 4, 8


def on_device(queries, prefix_keys, prefix_values, resp_keys, resp_values, segment_ids, out_weight):
    ways = lax.axis_size("mp")
    tokens, width = queries.shape
    group = width // HD
    rows = segment_ids.shape[0]
    quarter = rows // Y
    along_z = [[y * Z + z for z in range(Z)] for y in range(Y)]
    place = lax.axis_index("seq")

    def across_z(array):
        return lax.all_to_all(array, "seq", 0, 0, axis_index_groups=along_z, tiled=True)

    def along_y(array, step):
        pairs = [(y * Z + z, (y + step) % Y * Z + z) for y in range(Y) for z in range(Z)]
        return lax.ppermute(array, "seq", pairs)

    mine = across_z(jnp.broadcast_to(queries[None], (Z,) + queries.shape)).reshape(quarter, width)

    columns, own_columns, fact = prepare(prefix_values, resp_values)
    first = place * tokens
    own_segments = lax.dynamic_slice_in_dim(segment_ids, first, tokens)
    own_rows = first + jnp.arange(tokens, dtype=jnp.int32)
    allowed = (own_segments[:, None] == segment_ids[None, :]) & (
        own_rows[:, None] <= jnp.arange(rows, dtype=jnp.int32)[None, :]
    )
    bias = jnp.where(allowed, f32(0), f32(-1e30))

    def bias_for(step):
        owner = (place // Z + Y - step) % Y
        return lax.dynamic_slice_in_dim(bias, owner * quarter, quarter, 1)

    def part_for(array, block):
        return attend(array, prefix_keys, columns, resp_keys, own_columns, block, fact)

    blocks = [bias_for(step) for step in range(Y)]
    mine, columns, own_columns, fact, *blocks = lax.optimization_barrier(
        (mine, columns, own_columns, fact, *blocks)
    )
    arrivals = {step: along_y(mine, step) for step in (1, 3, 2)}
    own = [part_for(mine[:, : width // 2], blocks[0])]
    *blocks, own[0] = lax.optimization_barrier((*blocks, own[0]))
    parts = [along_y(part_for(arrivals[step], blocks[step]), -step) for step in (1, 2, 3)]
    own.append(part_for(mine[:, width // 2 :], blocks[0]))

    joined = across_z(join(own, parts, group, Z))
    heads = across_z(combine(joined, group)).reshape(quarter, width)
    pieces = [heads] + [along_y(heads, step) for step in (1, 3, 2)]
    scored = [
        jnp.dot(piece, out_weight, preferred_element_type=f32).astype(bf16) for piece in pieces
    ]
    order = (0, 1, 3, 2)
    whole = jnp.zeros((rows, out_weight.shape[1]), bf16)
    for step, piece in zip(order, scored):
        owner = (place // Z + Y - step) % Y
        whole = lax.dynamic_update_slice_in_dim(whole, piece, owner * quarter, 0)
    scored = whole.reshape(ways, rows // ways, -1)
    scored = lax.all_to_all(scored, "mp", 0, 0, tiled=True)
    return jnp.sum(scored.astype(f32), axis=0).astype(bf16)


def solution(mesh):
    in_specs = (
        P("seq", "mp"),
        P("seq", "mp"),
        P("seq", "mp"),
        P("seq", "mp"),
        P("seq", "mp"),
        P(),
        P("mp", "seq"),
    )
    return jax.shard_map(
        on_device, mesh=mesh, in_specs=in_specs, out_specs=P("mp", "seq"), check_vma=False
    )
```

```python
import jax
import jax.numpy as jnp
from jax import lax
from jax.experimental import pallas as pl
from jax.experimental.pallas import tpu as pltpu
from jax.sharding import PartitionSpec as P

HD = 128
SCALE2 = HD**-0.5 * 1.4426950408889634
LOWEST = 2.0**-60
HIGHEST = 2.0**100
SMALL = 2.0**-20
ONES = 16
DEPTH = 4
f32 = jnp.float32
bf16 = jnp.bfloat16


def split3(x):
    high = x.astype(bf16).astype(f32)
    rest = x - high
    middle = rest.astype(bf16).astype(f32)
    return high, middle, rest - middle


def prepare_kernel(v_ref, rv_ref, vt_ref, fact_ref):
    v = v_ref[...]
    vt_ref[:HD, :] = v.T
    vt_ref[HD:, :] = jnp.ones((ONES, v.shape[0]), bf16)
    fact_ref[0, 0] = jnp.maximum(
        jnp.max(jnp.abs(v.astype(f32))), jnp.max(jnp.abs(rv_ref[...].astype(f32)))
    )


def prepare(values, own_values):
    vmem = pl.BlockSpec(memory_space=pltpu.VMEM)
    return pl.pallas_call(
        prepare_kernel,
        out_shape=(
            jax.ShapeDtypeStruct((HD + ONES, values.shape[0]), bf16),
            jax.ShapeDtypeStruct((1, 1), f32),
        ),
        out_specs=(vmem, pl.BlockSpec(memory_space=pltpu.SMEM)),
        name="prepare",
    )(values, own_values)


def attend_kernel(
    group, stack, key_block, q_ref, k_ref, vt_ref, rk_ref, rv_ref, bias_ref, fact_ref, out_ref,
    logs_ref,
):
    tokens = q_ref.shape[0]
    keys = k_ref.shape[0]

    def scores(keys_block, q):
        return (
            lax.dot_general(
                keys_block, q, (((1,), (1,)), ((), ())), preferred_element_type=f32
            )
            * SCALE2
        )

    def product(columns, weights):
        return jnp.dot(columns, weights.astype(bf16), preferred_element_type=f32)

    def result_of(total):
        return (total[:HD] / total[HD : HD + 1]).T.astype(bf16)

    def logs_rows(rows):
        pieces = split3(jnp.concatenate(rows, axis=0))
        out_ref[group * tokens :, :] = jnp.concatenate(
            pieces + (jnp.zeros((group, tokens), f32),), axis=0
        ).astype(bf16)

    own_columns = jnp.concatenate(
        [rv_ref[...].T, jnp.ones((ONES, rv_ref.shape[0]), bf16)], axis=0
    )
    lowest, highest = [], []
    logs = []
    bias = jnp.concatenate([bias_ref[...]] * stack, axis=1)
    for first in range(0, group, stack):
        q = jnp.concatenate(
            [q_ref[:, head * HD : (head + 1) * HD] for head in range(first, first + stack)], axis=0
        )
        total = product(own_columns, jnp.exp2(scores(rk_ref[...], q) + bias))
        now = scores(k_ref[:key_block, :], q)
        for start in range(0, keys, key_block):
            later = start + key_block
            if later < keys:
                following = scores(k_ref[later : later + key_block, :], q)
            total += product(vt_ref[:, start:later], jnp.exp2(now))
            if later < keys:
                now = following
        sums = total[HD : HD + 1]
        lowest.append(jnp.min(sums))
        highest.append(jnp.max(sums))
        log = jnp.log2(sums)
        for at in range(stack):
            lanes = slice(at * tokens, (at + 1) * tokens)
            logs.append(log[:, lanes])
            head = first + at
            out_ref[head * tokens : (head + 1) * tokens, :] = result_of(total[:, lanes])
    logs_rows(logs)
    inside = fact_ref[0, 0] >= SMALL
    for low, high in zip(lowest, highest):
        inside = inside & (low >= LOWEST) & (high <= HIGHEST)

    @pl.when(jnp.logical_not(inside))
    def _():
        @pl.loop(0, group)
        def _(head):
            q = q_ref[:, pl.ds(pl.multiple_of(head * HD, HD), HD)]
            mine = scores(rk_ref[...], q) + bias_ref[...]
            rest = scores(k_ref[...], q)
            top = jnp.maximum(
                jnp.max(mine, axis=0, keepdims=True), jnp.max(rest, axis=0, keepdims=True)
            )
            total = product(own_columns, jnp.exp2(mine - top))
            total += product(vt_ref[...], jnp.exp2(rest - top))
            logs_ref[pl.ds(head, 1), :] = jnp.log2(total[HD : HD + 1]) + top
            out_ref[pl.ds(pl.multiple_of(head * tokens, tokens), tokens), :] = result_of(total)

        logs_rows([logs_ref[...]])


def attend(queries, keys, columns, own_keys, own_values, bias, fact):
    tokens, width = queries.shape
    group = width // HD
    vmem = pl.BlockSpec(memory_space=pltpu.VMEM)
    return pl.pallas_call(
        lambda *refs: attend_kernel(group, min(4, group), 512, *refs),
        out_shape=jax.ShapeDtypeStruct((group * (tokens + DEPTH), HD), bf16),
        in_specs=[vmem] * 6 + [pl.BlockSpec(memory_space=pltpu.SMEM)],
        out_specs=vmem,
        scratch_shapes=[pltpu.VMEM((group, tokens), f32)],
        compiler_params=pltpu.CompilerParams(vmem_limit_bytes=20 << 20),
        name="attend",
    )(queries, keys, columns, own_keys, own_values, bias, fact)


def join_kernel(group, halves, *refs):
    own_refs, part_refs, out_ref = refs[:halves], refs[halves:-1], refs[-1]
    owners = out_ref.shape[0]
    tokens = part_refs[0].shape[0] // group - DEPTH
    few = group // halves

    def log_of(ref, heads):
        pieces = ref[heads * tokens :, :].astype(f32)
        return sum(pieces[at * heads : (at + 1) * heads] for at in range(3))

    def part_of(at, head):
        ref = part_refs[at - 1] if at else own_refs[head // few]
        row = head * tokens if at else head % few * tokens
        return ref[row : row + tokens, :].astype(f32)

    logs = [jnp.concatenate([log_of(ref, few) for ref in own_refs], axis=0)]
    logs += [log_of(ref, group) for ref in part_refs]
    top = logs[0]
    for log in logs[1:]:
        top = jnp.maximum(top, log)
    shares = [jnp.exp2(log - top) for log in logs]
    whole = sum(shares)
    shares = [share / whole for share in shares]
    rows = list(split3(top + jnp.log2(whole))) + shares
    rows.append(jnp.zeros((HD - group * len(rows), tokens), f32))
    turned = jnp.concatenate(rows, axis=0).T
    split = tokens // owners
    for head in range(group):
        total = None
        for at in range(len(shares)):
            lane = (3 + at) * group + head
            term = part_of(at, head) * turned[:, lane : lane + 1]
            total = term if total is None else total + term
        out_ref[:, head * split : (head + 1) * split, :] = total.astype(bf16).reshape(
            owners, split, HD
        )
    out_ref[:, group * split :, :] = turned.astype(bf16).reshape(owners, split, HD)


def join(own, parts, group, owners):
    tokens = parts[0].shape[0] // group - DEPTH
    return pl.pallas_call(
        lambda *refs: join_kernel(group, len(own), *refs),
        out_shape=jax.ShapeDtypeStruct((owners, (group + 1) * (tokens // owners), HD), bf16),
        compiler_params=pltpu.CompilerParams(vmem_limit_bytes=20 << 20),
        name="join",
    )(*own, *parts)


def combine_kernel(group, parts_ref, out_ref):
    copies, tokens, _ = out_ref.shape
    pieces = parts_ref[:, group * tokens :, :].astype(f32)
    logs = sum(pieces[:, :, piece * group : (piece + 1) * group] for piece in range(3))
    share = jnp.exp2(logs - jnp.max(logs, axis=0, keepdims=True))
    share = share / jnp.sum(share, axis=0, keepdims=True)
    for head in range(group):
        part = parts_ref[:, head * tokens : (head + 1) * tokens, :].astype(f32)
        result = jnp.sum(part * share[:, :, head : head + 1], axis=0).astype(bf16)
        out_ref[:, :, head * HD : (head + 1) * HD] = jnp.broadcast_to(
            result[None], (copies, tokens, HD)
        )


def combine(parts, group):
    owners, height, _ = parts.shape
    return pl.pallas_call(
        lambda *refs: combine_kernel(group, *refs),
        out_shape=jax.ShapeDtypeStruct((owners, height // (group + 1), group * HD), bf16),
        compiler_params=pltpu.CompilerParams(vmem_limit_bytes=20 << 20),
        name="combine",
    )(parts)


def project_kernel(side_ref, heads_ref, *refs):
    weight_refs, out_ref = refs[:-1], refs[-1]
    heads = heads_ref[...]
    sides = len(weight_refs)
    rows = out_ref.shape[1]
    for step, ref in enumerate(weight_refs):
        column = lax.rem(side_ref[0] + sides - step, sides)
        block = jnp.dot(heads, ref[...], preferred_element_type=f32).astype(bf16)
        for half in range(out_ref.shape[0] // sides):
            out_ref[half * sides + column] = block[half * rows : (half + 1) * rows]


def project(side, heads, weights, ways):
    rows = heads.shape[0] * len(weights) // ways
    vmem = pl.BlockSpec(memory_space=pltpu.VMEM)
    return pl.pallas_call(
        project_kernel,
        out_shape=jax.ShapeDtypeStruct((ways, rows, weights[0].shape[1]), bf16),
        in_specs=[pl.BlockSpec(memory_space=pltpu.SMEM)] + [vmem] * (1 + len(weights)),
        out_specs=vmem,
        compiler_params=pltpu.CompilerParams(vmem_limit_bytes=20 << 20),
        name="project",
    )(side, heads, *weights)


Y, Z = 4, 8


def on_device(queries, prefix_keys, prefix_values, resp_keys, resp_values, segment_ids, out_weight):
    ways = lax.axis_size("mp")
    tokens, width = queries.shape
    group = width // HD
    rows = segment_ids.shape[0]
    quarter = rows // Y
    along_z = [[y * Z + z for z in range(Z)] for y in range(Y)]
    place = lax.axis_index("seq")

    def across_z(array):
        return lax.all_to_all(array, "seq", 0, 0, axis_index_groups=along_z, tiled=True)

    def along_y(array, step):
        pairs = [(y * Z + z, (y + step) % Y * Z + z) for y in range(Y) for z in range(Z)]
        return lax.ppermute(array, "seq", pairs)

    mine = across_z(jnp.broadcast_to(queries[None], (Z,) + queries.shape)).reshape(quarter, width)

    columns, fact = prepare(prefix_values, resp_values)
    first = place * tokens
    own_segments = lax.dynamic_slice_in_dim(segment_ids, first, tokens)
    own_rows = first + jnp.arange(tokens, dtype=jnp.int32)
    allowed = (own_segments[:, None] == segment_ids[None, :]) & (
        own_rows[:, None] <= jnp.arange(rows, dtype=jnp.int32)[None, :]
    )
    bias = jnp.where(allowed, f32(0), f32(-1e30))

    def bias_for(step):
        owner = (place // Z + Y - step) % Y
        return lax.dynamic_slice_in_dim(bias, owner * quarter, quarter, 1)

    def part_for(array, block):
        return attend(array, prefix_keys, columns, resp_keys, resp_values, block, fact)

    blocks = [bias_for(step) for step in range(Y)]
    mine, columns, fact, *blocks = lax.optimization_barrier((mine, columns, fact, *blocks))
    arrivals = {step: along_y(mine, step) for step in (1, 3, 2)}
    own = [part_for(mine[:, : width // 2], blocks[0])]
    *blocks, own[0] = lax.optimization_barrier((*blocks, own[0]))
    parts = [along_y(part_for(arrivals[step], blocks[step]), -step) for step in (1, 2, 3)]
    own.append(part_for(mine[:, width // 2 :], blocks[0]))

    out_weight, own[1] = lax.optimization_barrier((out_weight, own[1]))
    weights = [out_weight] + [along_y(out_weight, step) for step in (1, 2, 3)]
    joined = across_z(join(own, parts, group, Z))
    heads = across_z(combine(joined, group)).reshape(quarter, width)
    side = (place // Z).astype(jnp.int32).reshape(1)
    scored = lax.all_to_all(project(side, heads, weights, ways), "mp", 0, 0, tiled=True)
    scored = jnp.sum(scored.astype(f32), axis=0).astype(bf16)
    pairs = []
    for y in range(Y):
        for z in range(Z):
            for block in range(ways):
                half, column = block // Y, block % Y
                source = (y * Z + z) * ways + block
                pairs.append((source, (column * Z + z) * ways + y * (ways // Y) + half))
    return lax.ppermute(scored, ("seq", "mp"), pairs)


def solution(mesh):
    in_specs = (
        P("seq", "mp"),
        P("seq", "mp"),
        P("seq", "mp"),
        P("seq", "mp"),
        P("seq", "mp"),
        P(),
        P("mp", "seq"),
    )
    return jax.shard_map(
        on_device, mesh=mesh, in_specs=in_specs, out_specs=P("mp", "seq"), check_vma=False
    )
```

```python
import jax
import jax.numpy as jnp
from jax import lax
from jax.experimental import pallas as pl
from jax.experimental.pallas import tpu as pltpu
from jax.sharding import PartitionSpec as P

HD = 128
SCALE2 = HD**-0.5 * 1.4426950408889634
LOWEST = 2.0**-60
HIGHEST = 2.0**100
SMALL = 2.0**-20
DEPTH = 4
f32 = jnp.float32
bf16 = jnp.bfloat16


def split3(x):
    high = x.astype(bf16).astype(f32)
    rest = x - high
    middle = rest.astype(bf16).astype(f32)
    return high, middle, rest - middle


def prepare_kernel(v_ref, rv_ref, vt_ref, fact_ref):
    v = v_ref[...]
    vt_ref[...] = v.T
    fact_ref[0, 0] = jnp.maximum(
        jnp.max(jnp.abs(v.astype(f32))), jnp.max(jnp.abs(rv_ref[...].astype(f32)))
    )


def prepare(values, own_values):
    vmem = pl.BlockSpec(memory_space=pltpu.VMEM)
    return pl.pallas_call(
        prepare_kernel,
        out_shape=(
            pltpu.VMEM((HD, values.shape[0]), bf16),
            jax.ShapeDtypeStruct((1, 1), f32),
        ),
        out_specs=(vmem, pl.BlockSpec(memory_space=pltpu.SMEM)),
        compiler_params=pltpu.CompilerParams(vmem_limit_bytes=20 << 20),
        name="prepare",
    )(values, own_values)


def replicate_kernel(x_ref, out_ref, sems):
    moves = [
        pltpu.make_async_copy(x_ref, out_ref.at[at], sems.at[at]) for at in range(out_ref.shape[0])
    ]
    for move in moves:
        move.start()
    for move in moves:
        move.wait()


def replicate(array, count):
    return pl.pallas_call(
        replicate_kernel,
        out_shape=jax.ShapeDtypeStruct((count,) + array.shape, array.dtype),
        in_specs=[pl.BlockSpec(memory_space=pltpu.VMEM)],
        out_specs=pl.BlockSpec(memory_space=pl.ANY),
        scratch_shapes=[pltpu.SemaphoreType.DMA((count,))],
        compiler_params=pltpu.CompilerParams(vmem_limit_bytes=20 << 20),
        name="replicate",
    )(array)


def attend_kernel(
    group, stack, key_block, q_ref, k_ref, vt_ref, rk_ref, rv_ref, bias_ref, fact_ref, out_ref,
    logs_ref,
):
    tokens = q_ref.shape[0]
    keys = k_ref.shape[0]

    def scores(keys_block, q):
        return (
            lax.dot_general(
                keys_block, q, (((1,), (1,)), ((), ())), preferred_element_type=f32
            )
            * SCALE2
        )

    def product(columns, weights):
        return jnp.dot(columns, weights.astype(bf16), preferred_element_type=f32)

    def result_of(total, sums):
        return (total / sums).T.astype(bf16)

    def logs_rows(rows):
        pieces = split3(jnp.concatenate(rows, axis=0))
        out_ref[group * tokens :, :] = jnp.concatenate(
            pieces + (jnp.zeros((group, tokens), f32),), axis=0
        ).astype(bf16)

    def fold(weights):
        return jnp.sum(weights.reshape(-1, 8, weights.shape[1]), axis=0)

    own_columns = rv_ref[...].T
    everything, logs = [], []
    bias = jnp.concatenate([bias_ref[...]] * stack, axis=1)
    for first in range(0, group, stack):
        q = jnp.concatenate(
            [q_ref[:, head * HD : (head + 1) * HD] for head in range(first, first + stack)], axis=0
        )
        total, sums = None, None
        now = scores(k_ref[:key_block, :], q)
        for start in range(0, keys, key_block):
            later = start + key_block
            if later < keys:
                following = scores(k_ref[later : later + key_block, :], q)
            else:
                following = scores(rk_ref[...], q) + bias
            weights = jnp.exp2(now)
            term = product(vt_ref[:, start:later], weights)
            total = term if total is None else total + term
            sums = fold(weights) if sums is None else sums + fold(weights)
            now = following
        weights = jnp.exp2(now)
        total += product(own_columns, weights)
        sums = jnp.sum(sums + fold(weights), axis=0, keepdims=True)
        everything.append(sums)
        log = jnp.log2(sums)
        for at in range(stack):
            lanes = slice(at * tokens, (at + 1) * tokens)
            logs.append(log[:, lanes])
            head = first + at
            out_ref[head * tokens : (head + 1) * tokens, :] = result_of(
                total[:, lanes], sums[:, lanes]
            )
    logs_rows(logs)
    sums = jnp.concatenate(everything, axis=1)
    outside = jnp.where((sums >= LOWEST) & (sums <= HIGHEST), f32(0), f32(1))
    inside = (jnp.max(outside) < 0.5) & (fact_ref[0, 0] >= SMALL)

    @pl.when(jnp.logical_not(inside))
    def _():
        @pl.loop(0, group)
        def _(head):
            q = q_ref[:, pl.ds(pl.multiple_of(head * HD, HD), HD)]
            mine = scores(rk_ref[...], q) + bias_ref[...]
            rest = scores(k_ref[...], q)
            top = jnp.maximum(
                jnp.max(mine, axis=0, keepdims=True), jnp.max(rest, axis=0, keepdims=True)
            )
            mine, rest = jnp.exp2(mine - top), jnp.exp2(rest - top)
            total = product(own_columns, mine) + product(vt_ref[...], rest)
            sums = jnp.sum(mine, axis=0, keepdims=True) + jnp.sum(rest, axis=0, keepdims=True)
            logs_ref[pl.ds(head, 1), :] = jnp.log2(sums) + top
            out_ref[pl.ds(pl.multiple_of(head * tokens, tokens), tokens), :] = result_of(
                total, sums
            )

        logs_rows([logs_ref[...]])


def attend(queries, keys, columns, own_keys, own_values, bias, fact):
    tokens, width = queries.shape
    group = width // HD
    vmem = pl.BlockSpec(memory_space=pltpu.VMEM)
    return pl.pallas_call(
        lambda *refs: attend_kernel(group, min(4, group), 512, *refs),
        out_shape=jax.ShapeDtypeStruct((group * (tokens + DEPTH), HD), bf16),
        in_specs=[vmem] * 6 + [pl.BlockSpec(memory_space=pltpu.SMEM)],
        out_specs=vmem,
        scratch_shapes=[pltpu.VMEM((group, tokens), f32)],
        compiler_params=pltpu.CompilerParams(vmem_limit_bytes=20 << 20),
        name="attend",
    )(queries, keys, columns, own_keys, own_values, bias, fact)


def join_kernel(group, halves, *refs):
    own_refs, part_refs, out_ref = refs[:halves], refs[halves:-1], refs[-1]
    owners = out_ref.shape[0]
    tokens = part_refs[0].shape[0] // group - DEPTH
    few = group // halves

    def log_of(ref, heads):
        pieces = ref[heads * tokens :, :].astype(f32)
        return sum(pieces[at * heads : (at + 1) * heads] for at in range(3))

    def part_of(at, head):
        ref = part_refs[at - 1] if at else own_refs[head // few]
        row = head * tokens if at else head % few * tokens
        return ref[row : row + tokens, :].astype(f32)

    logs = [jnp.concatenate([log_of(ref, few) for ref in own_refs], axis=0)]
    logs += [log_of(ref, group) for ref in part_refs]
    top = logs[0]
    for log in logs[1:]:
        top = jnp.maximum(top, log)
    shares = [jnp.exp2(log - top) for log in logs]
    whole = sum(shares)
    shares = [share / whole for share in shares]
    rows = list(split3(top + jnp.log2(whole))) + shares
    rows.append(jnp.zeros((HD - group * len(rows), tokens), f32))
    turned = jnp.concatenate(rows, axis=0).T
    split = tokens // owners
    for head in range(group):
        total = None
        for at in range(len(shares)):
            lane = (3 + at) * group + head
            term = part_of(at, head) * turned[:, lane : lane + 1]
            total = term if total is None else total + term
        out_ref[:, head * split : (head + 1) * split, :] = total.astype(bf16).reshape(
            owners, split, HD
        )
    out_ref[:, group * split :, :] = turned.astype(bf16).reshape(owners, split, HD)


def join(own, parts, group, owners):
    tokens = parts[0].shape[0] // group - DEPTH
    return pl.pallas_call(
        lambda *refs: join_kernel(group, len(own), *refs),
        out_shape=jax.ShapeDtypeStruct((owners, (group + 1) * (tokens // owners), HD), bf16),
        compiler_params=pltpu.CompilerParams(vmem_limit_bytes=20 << 20),
        name="join",
    )(*own, *parts)


def combine_kernel(group, parts_ref, out_ref):
    copies, tokens, _ = out_ref.shape
    pieces = parts_ref[:, group * tokens :, :].astype(f32)
    logs = sum(pieces[:, :, piece * group : (piece + 1) * group] for piece in range(3))
    share = jnp.exp2(logs - jnp.max(logs, axis=0, keepdims=True))
    share = share / jnp.sum(share, axis=0, keepdims=True)
    for head in range(group):
        part = parts_ref[:, head * tokens : (head + 1) * tokens, :].astype(f32)
        result = jnp.sum(part * share[:, :, head : head + 1], axis=0).astype(bf16)
        out_ref[:, :, head * HD : (head + 1) * HD] = jnp.broadcast_to(
            result[None], (copies, tokens, HD)
        )


def combine(parts, group):
    owners, height, _ = parts.shape
    return pl.pallas_call(
        lambda *refs: combine_kernel(group, *refs),
        out_shape=jax.ShapeDtypeStruct((owners, height // (group + 1), group * HD), bf16),
        compiler_params=pltpu.CompilerParams(vmem_limit_bytes=20 << 20),
        name="combine",
    )(parts)


def project_kernel(heads_ref, *refs):
    sides = len(refs) // 2
    heads = heads_ref[...]
    for weight_ref, out_ref in zip(refs[:sides], refs[sides:]):
        out_ref[...] = jnp.dot(heads, weight_ref[...], preferred_element_type=f32).astype(bf16)


def project(heads, weights):
    vmem = pl.BlockSpec(memory_space=pltpu.VMEM)
    shape = jax.ShapeDtypeStruct((heads.shape[0], weights[0].shape[1]), bf16)
    return pl.pallas_call(
        project_kernel,
        out_shape=(shape,) * len(weights),
        out_specs=(vmem,) * len(weights),
        compiler_params=pltpu.CompilerParams(vmem_limit_bytes=20 << 20),
        name="project",
    )(heads, *weights)


def place_rows_kernel(side_ref, *refs):
    block_refs, out_ref = refs[:-1], refs[-1]
    sides = len(block_refs)
    rows = out_ref.shape[1]
    per = out_ref.shape[0] // sides
    for step, ref in enumerate(block_refs):
        owner = lax.rem(side_ref[0] + step, sides)
        for half in range(per):
            out_ref[owner * per + half] = ref[half * rows : (half + 1) * rows, :]


def place_rows(side, blocks, ways):
    vmem = pl.BlockSpec(memory_space=pltpu.VMEM)
    rows = len(blocks) * blocks[0].shape[0] // ways
    return pl.pallas_call(
        place_rows_kernel,
        out_shape=jax.ShapeDtypeStruct((ways, rows, blocks[0].shape[1]), bf16),
        in_specs=[pl.BlockSpec(memory_space=pltpu.SMEM)] + [vmem] * len(blocks),
        out_specs=vmem,
        compiler_params=pltpu.CompilerParams(vmem_limit_bytes=20 << 20),
        name="place_rows",
    )(side, *blocks)


Y, Z = 4, 8


def on_device(queries, prefix_keys, prefix_values, resp_keys, resp_values, segment_ids, out_weight):
    ways = lax.axis_size("mp")
    tokens, width = queries.shape
    group = width // HD
    rows = segment_ids.shape[0]
    quarter = rows // Y
    along_z = [[y * Z + z for z in range(Z)] for y in range(Y)]
    place = lax.axis_index("seq")

    def across_z(array):
        return lax.all_to_all(array, "seq", 0, 0, axis_index_groups=along_z, tiled=True)

    def along_y(array, step):
        pairs = [(y * Z + z, (y + step) % Y * Z + z) for y in range(Y) for z in range(Z)]
        return lax.ppermute(array, "seq", pairs)

    mine = across_z(replicate(queries, Z)).reshape(quarter, width)

    columns, fact = prepare(prefix_values, resp_values)
    first = place * tokens
    own_segments = lax.dynamic_slice_in_dim(segment_ids, first, tokens)
    own_rows = first + jnp.arange(tokens, dtype=jnp.int32)
    allowed = (own_segments[:, None] == segment_ids[None, :]) & (
        own_rows[:, None] <= jnp.arange(rows, dtype=jnp.int32)[None, :]
    )
    bias = jnp.where(allowed, f32(0), f32(-1e30))

    def bias_for(step):
        owner = (place // Z + Y - step) % Y
        return lax.dynamic_slice_in_dim(bias, owner * quarter, quarter, 1)

    def part_for(array, block):
        return attend(array, prefix_keys, columns, resp_keys, resp_values, block, fact)

    blocks = [bias_for(step) for step in range(Y)]
    mine, columns, fact, *blocks = lax.optimization_barrier((mine, columns, fact, *blocks))
    arrivals = {step: along_y(mine, step) for step in (1, 3, 2)}
    own = [part_for(mine[:, : width // 2], blocks[0])]
    *blocks, own[0] = lax.optimization_barrier((*blocks, own[0]))
    parts = [along_y(part_for(arrivals[step], blocks[step]), -step) for step in (1, 2, 3)]
    own.append(part_for(mine[:, width // 2 :], blocks[0]))

    out_weight, own[1] = lax.optimization_barrier((out_weight, own[1]))
    weights = [out_weight] + [along_y(out_weight, step) for step in (1, 2, 3)]
    joined = across_z(join(own, parts, group, Z))
    heads = across_z(combine(joined, group)).reshape(quarter, width)
    blocks = project(heads, weights)
    side = (place // Z).astype(jnp.int32).reshape(1)
    blocks = [blocks[0]] + [along_y(blocks[step], -step) for step in (1, 2, 3)]
    scored = lax.all_to_all(place_rows(side, blocks, ways), "mp", 0, 0, tiled=True)
    return jnp.sum(scored.astype(f32), axis=0).astype(bf16)


def solution(mesh):
    in_specs = (
        P("seq", "mp"),
        P("seq", "mp"),
        P("seq", "mp"),
        P("seq", "mp"),
        P("seq", "mp"),
        P(),
        P("mp", "seq"),
    )
    return jax.shard_map(
        on_device, mesh=mesh, in_specs=in_specs, out_specs=P("mp", "seq"), check_vma=False
    )
```

```python
import jax
import jax.numpy as jnp
from jax import lax
from jax.experimental import pallas as pl
from jax.experimental.pallas import tpu as pltpu
from jax.sharding import PartitionSpec as P

HD = 128
SCALE2 = HD**-0.5 * 1.4426950408889634
LOWEST = 2.0**-60
HIGHEST = 2.0**100
SMALL = 2.0**-20
DEPTH = 4
f32 = jnp.float32
bf16 = jnp.bfloat16


def split3(x):
    high = x.astype(bf16).astype(f32)
    rest = x - high
    middle = rest.astype(bf16).astype(f32)
    return high, middle, rest - middle


def prepare_kernel(v_ref, rv_ref, vt_ref, fact_ref):
    v = v_ref[...]
    vt_ref[...] = v.T
    fact_ref[0, 0] = jnp.maximum(
        jnp.max(jnp.abs(v.astype(f32))), jnp.max(jnp.abs(rv_ref[...].astype(f32)))
    )


def prepare(values, own_values):
    vmem = pl.BlockSpec(memory_space=pltpu.VMEM)
    return pl.pallas_call(
        prepare_kernel,
        out_shape=(
            pltpu.VMEM((HD, values.shape[0]), bf16),
            jax.ShapeDtypeStruct((1, 1), f32),
        ),
        out_specs=(vmem, pl.BlockSpec(memory_space=pltpu.SMEM)),
        compiler_params=pltpu.CompilerParams(vmem_limit_bytes=20 << 20),
        name="prepare",
    )(values, own_values)


def replicate_kernel(x_ref, out_ref, sems):
    moves = [
        pltpu.make_async_copy(x_ref, out_ref.at[at], sems.at[at]) for at in range(out_ref.shape[0])
    ]
    for move in moves:
        move.start()
    for move in moves:
        move.wait()


def replicate(array, count):
    return pl.pallas_call(
        replicate_kernel,
        out_shape=jax.ShapeDtypeStruct((count,) + array.shape, array.dtype),
        in_specs=[pl.BlockSpec(memory_space=pltpu.VMEM)],
        out_specs=pl.BlockSpec(memory_space=pl.ANY),
        scratch_shapes=[pltpu.SemaphoreType.DMA((count,))],
        compiler_params=pltpu.CompilerParams(vmem_limit_bytes=20 << 20),
        name="replicate",
    )(array)


def attend_kernel(
    group, stack, key_block, q_ref, k_ref, vt_ref, rk_ref, rv_ref, bias_ref, fact_ref, out_ref,
    logs_ref,
):
    tokens = q_ref.shape[0]
    keys = k_ref.shape[0]

    def scores(keys_block, q):
        return (
            lax.dot_general(
                keys_block, q, (((1,), (1,)), ((), ())), preferred_element_type=f32
            )
            * SCALE2
        )

    def product(columns, weights):
        return jnp.dot(columns, weights.astype(bf16), preferred_element_type=f32)

    def result_of(total, sums):
        return (total / sums).T.astype(bf16)

    def logs_rows(rows):
        pieces = split3(jnp.concatenate(rows, axis=0))
        out_ref[group * tokens :, :] = jnp.concatenate(
            pieces + (jnp.zeros((group, tokens), f32),), axis=0
        ).astype(bf16)

    def fold(weights):
        return jnp.sum(weights.reshape(-1, 8, weights.shape[1]), axis=0)

    own_columns = rv_ref[...].T
    everything, logs = [], []
    bias = jnp.concatenate([bias_ref[...]] * stack, axis=1)
    for first in range(0, group, stack):
        q = jnp.concatenate(
            [q_ref[:, head * HD : (head + 1) * HD] for head in range(first, first + stack)], axis=0
        )
        total, sums = None, None
        now = scores(k_ref[:key_block, :], q)
        for start in range(0, keys, key_block):
            later = start + key_block
            if later < keys:
                following = scores(k_ref[later : later + key_block, :], q)
            else:
                following = scores(rk_ref[...], q) + bias
            weights = jnp.exp2(now)
            term = product(vt_ref[:, start:later], weights)
            total = term if total is None else total + term
            sums = fold(weights) if sums is None else sums + fold(weights)
            now = following
        weights = jnp.exp2(now)
        total += product(own_columns, weights)
        sums = jnp.sum(sums + fold(weights), axis=0, keepdims=True)
        everything.append(sums)
        log = jnp.log2(sums)
        for at in range(stack):
            lanes = slice(at * tokens, (at + 1) * tokens)
            logs.append(log[:, lanes])
            head = first + at
            out_ref[head * tokens : (head + 1) * tokens, :] = result_of(
                total[:, lanes], sums[:, lanes]
            )
    logs_rows(logs)
    sums = jnp.concatenate(everything, axis=1)
    outside = jnp.where((sums >= LOWEST) & (sums <= HIGHEST), f32(0), f32(1))
    inside = (jnp.max(outside) < 0.5) & (fact_ref[0, 0] >= SMALL)

    @pl.when(jnp.logical_not(inside))
    def _():
        @pl.loop(0, group)
        def _(head):
            q = q_ref[:, pl.ds(pl.multiple_of(head * HD, HD), HD)]
            mine = scores(rk_ref[...], q) + bias_ref[...]
            rest = scores(k_ref[...], q)
            top = jnp.maximum(
                jnp.max(mine, axis=0, keepdims=True), jnp.max(rest, axis=0, keepdims=True)
            )
            mine, rest = jnp.exp2(mine - top), jnp.exp2(rest - top)
            total = product(own_columns, mine) + product(vt_ref[...], rest)
            sums = jnp.sum(mine, axis=0, keepdims=True) + jnp.sum(rest, axis=0, keepdims=True)
            logs_ref[pl.ds(head, 1), :] = jnp.log2(sums) + top
            out_ref[pl.ds(pl.multiple_of(head * tokens, tokens), tokens), :] = result_of(
                total, sums
            )

        logs_rows([logs_ref[...]])


def attend(queries, keys, columns, own_keys, own_values, bias, fact):
    tokens, width = queries.shape
    group = width // HD
    vmem = pl.BlockSpec(memory_space=pltpu.VMEM)
    return pl.pallas_call(
        lambda *refs: attend_kernel(group, min(4, group), 512, *refs),
        out_shape=jax.ShapeDtypeStruct((group * (tokens + DEPTH), HD), bf16),
        in_specs=[vmem] * 6 + [pl.BlockSpec(memory_space=pltpu.SMEM)],
        out_specs=vmem,
        scratch_shapes=[pltpu.VMEM((group, tokens), f32)],
        compiler_params=pltpu.CompilerParams(vmem_limit_bytes=20 << 20),
        name="attend",
    )(queries, keys, columns, own_keys, own_values, bias, fact)


def join_kernel(group, halves, *refs):
    own_refs, part_refs, out_ref = refs[:halves], refs[halves:-1], refs[-1]
    owners = out_ref.shape[0]
    tokens = part_refs[0].shape[0] // group - DEPTH
    few = group // halves

    def log_of(ref, heads):
        pieces = ref[heads * tokens :, :].astype(f32)
        return sum(pieces[at * heads : (at + 1) * heads] for at in range(3))

    def part_of(at, head):
        ref = part_refs[at - 1] if at else own_refs[head // few]
        row = head * tokens if at else head % few * tokens
        return ref[row : row + tokens, :].astype(f32)

    logs = [jnp.concatenate([log_of(ref, few) for ref in own_refs], axis=0)]
    logs += [log_of(ref, group) for ref in part_refs]
    top = logs[0]
    for log in logs[1:]:
        top = jnp.maximum(top, log)
    shares = [jnp.exp2(log - top) for log in logs]
    whole = sum(shares)
    shares = [share / whole for share in shares]
    rows = list(split3(top + jnp.log2(whole))) + shares
    rows.append(jnp.zeros((HD - group * len(rows), tokens), f32))
    turned = jnp.concatenate(rows, axis=0).T
    split = tokens // owners
    for head in range(group):
        total = None
        for at in range(len(shares)):
            lane = (3 + at) * group + head
            term = part_of(at, head) * turned[:, lane : lane + 1]
            total = term if total is None else total + term
        out_ref[:, head * split : (head + 1) * split, :] = total.astype(bf16).reshape(
            owners, split, HD
        )
    out_ref[:, group * split :, :] = turned.astype(bf16).reshape(owners, split, HD)


def join(own, parts, group, owners):
    tokens = parts[0].shape[0] // group - DEPTH
    return pl.pallas_call(
        lambda *refs: join_kernel(group, len(own), *refs),
        out_shape=jax.ShapeDtypeStruct((owners, (group + 1) * (tokens // owners), HD), bf16),
        compiler_params=pltpu.CompilerParams(vmem_limit_bytes=20 << 20),
        name="join",
    )(*own, *parts)


def combine_kernel(group, parts_ref, out_ref):
    copies, tokens, _ = out_ref.shape
    pieces = parts_ref[:, group * tokens :, :].astype(f32)
    logs = sum(pieces[:, :, piece * group : (piece + 1) * group] for piece in range(3))
    share = jnp.exp2(logs - jnp.max(logs, axis=0, keepdims=True))
    share = share / jnp.sum(share, axis=0, keepdims=True)
    for head in range(group):
        part = parts_ref[:, head * tokens : (head + 1) * tokens, :].astype(f32)
        result = jnp.sum(part * share[:, :, head : head + 1], axis=0).astype(bf16)
        out_ref[:, :, head * HD : (head + 1) * HD] = jnp.broadcast_to(
            result[None], (copies, tokens, HD)
        )


def combine(parts, group):
    owners, height, _ = parts.shape
    return pl.pallas_call(
        lambda *refs: combine_kernel(group, *refs),
        out_shape=jax.ShapeDtypeStruct((owners, height // (group + 1), group * HD), bf16),
        compiler_params=pltpu.CompilerParams(vmem_limit_bytes=20 << 20),
        name="combine",
    )(parts)


def project_kernel(at_ref, heads_ref, *refs):
    held = refs[-1]
    ways, rows, _ = held.shape
    weight_refs, out_refs = refs[: -1 - ways], refs[-1 - ways : -1]
    heads = heads_ref[...]
    sides = len(weight_refs)
    for step, ref in enumerate(weight_refs):
        column = lax.rem(at_ref[0] + sides - step, sides)
        block = jnp.dot(heads, ref[...], preferred_element_type=f32).astype(bf16)
        for half in range(ways // sides):
            held[half * sides + column] = block[half * rows : (half + 1) * rows]
    for step, ref in enumerate(out_refs):
        ref[...] = held[lax.rem(at_ref[1] + step, ways)]


def project(at, heads, weights, ways):
    vmem = pl.BlockSpec(memory_space=pltpu.VMEM)
    shape = (heads.shape[0] * len(weights) // ways, weights[0].shape[1])
    return pl.pallas_call(
        project_kernel,
        out_shape=(jax.ShapeDtypeStruct(shape, bf16),) * ways,
        in_specs=[pl.BlockSpec(memory_space=pltpu.SMEM)] + [vmem] * (1 + len(weights)),
        out_specs=(vmem,) * ways,
        scratch_shapes=[pltpu.VMEM((ways,) + shape, bf16)],
        compiler_params=pltpu.CompilerParams(vmem_limit_bytes=20 << 20),
        name="project",
    )(at, heads, *weights)


def total_kernel(*refs):
    total = refs[0][...].astype(f32)
    for ref in refs[1:-1]:
        total += ref[...].astype(f32)
    refs[-1][...] = total.astype(bf16)


def total_of(blocks):
    return pl.pallas_call(
        total_kernel,
        out_shape=jax.ShapeDtypeStruct(blocks[0].shape, bf16),
        compiler_params=pltpu.CompilerParams(vmem_limit_bytes=20 << 20),
        name="total",
    )(*blocks)


Y, Z = 4, 8


def on_device(queries, prefix_keys, prefix_values, resp_keys, resp_values, segment_ids, out_weight):
    ways = lax.axis_size("mp")
    tokens, width = queries.shape
    group = width // HD
    rows = segment_ids.shape[0]
    quarter = rows // Y
    along_z = [[y * Z + z for z in range(Z)] for y in range(Y)]
    place = lax.axis_index("seq")

    def across_z(array):
        return lax.all_to_all(array, "seq", 0, 0, axis_index_groups=along_z, tiled=True)

    def along_y(array, step):
        pairs = [(y * Z + z, (y + step) % Y * Z + z) for y in range(Y) for z in range(Z)]
        return lax.ppermute(array, "seq", pairs)

    mine = across_z(replicate(queries, Z)).reshape(quarter, width)

    columns, fact = prepare(prefix_values, resp_values)
    first = place * tokens
    own_segments = lax.dynamic_slice_in_dim(segment_ids, first, tokens)
    own_rows = first + jnp.arange(tokens, dtype=jnp.int32)
    allowed = (own_segments[:, None] == segment_ids[None, :]) & (
        own_rows[:, None] <= jnp.arange(rows, dtype=jnp.int32)[None, :]
    )
    bias = jnp.where(allowed, f32(0), f32(-1e30))

    def bias_for(step):
        owner = (place // Z + Y - step) % Y
        return lax.dynamic_slice_in_dim(bias, owner * quarter, quarter, 1)

    def part_for(array, block):
        return attend(array, prefix_keys, columns, resp_keys, resp_values, block, fact)

    blocks = [bias_for(step) for step in range(Y)]
    mine, columns, fact, *blocks = lax.optimization_barrier((mine, columns, fact, *blocks))
    arrivals = {step: along_y(mine, step) for step in (1, 3, 2)}
    own = [part_for(mine[:, : width // 2], blocks[0])]
    *blocks, own[0] = lax.optimization_barrier((*blocks, own[0]))
    parts = [along_y(part_for(arrivals[step], blocks[step]), -step) for step in (1, 2, 3)]
    own.append(part_for(mine[:, width // 2 :], blocks[0]))

    out_weight, own[1] = lax.optimization_barrier((out_weight, own[1]))
    weights = [out_weight] + [along_y(out_weight, step) for step in (1, 2, 3)]
    joined = across_z(join(own, parts, group, Z))
    heads = across_z(combine(joined, group)).reshape(quarter, width)
    at = jnp.stack([place // Z, lax.axis_index("mp")]).astype(jnp.int32)
    blocks = []
    for step, block in enumerate(project(at, heads, weights, ways)):
        pairs = []
        for y in range(Y):
            for z in range(Z):
                for m in range(ways):
                    half, column = divmod((m + step) % ways, Y)
                    target = (column * Z + z) * ways + y * (ways // Y) + half
                    pairs.append(((y * Z + z) * ways + m, target))
        blocks.append(lax.ppermute(block, ("seq", "mp"), pairs))
    return total_of(blocks)


def solution(mesh):
    in_specs = (
        P("seq", "mp"),
        P("seq", "mp"),
        P("seq", "mp"),
        P("seq", "mp"),
        P("seq", "mp"),
        P(),
        P("mp", "seq"),
    )
    return jax.shard_map(
        on_device, mesh=mesh, in_specs=in_specs, out_specs=P("mp", "seq"), check_vma=False
    )
```

```python
import jax
import jax.numpy as jnp
from jax import lax
from jax.experimental import pallas as pl
from jax.experimental.pallas import tpu as pltpu
from jax.sharding import PartitionSpec as P

HD = 128
SCALE2 = HD**-0.5 * 1.4426950408889634
LOWEST = 2.0**-60
HIGHEST = 2.0**100
SMALL = 2.0**-20
DEPTH = 4
f32 = jnp.float32
bf16 = jnp.bfloat16


def split3(x):
    high = x.astype(bf16).astype(f32)
    rest = x - high
    middle = rest.astype(bf16).astype(f32)
    return high, middle, rest - middle


def prepare_kernel(v_ref, rk_ref, rv_ref, vt_ref, rk_out_ref, rvt_ref, fact_ref):
    v, rv = v_ref[...], rv_ref[...]
    vt_ref[...] = v.T
    rk_out_ref[...] = rk_ref[...]
    rvt_ref[...] = rv.T
    fact_ref[0, 0] = jnp.maximum(
        jnp.max(jnp.abs(v.astype(f32))), jnp.max(jnp.abs(rv.astype(f32)))
    )


def prepare(values, own_keys, own_values):
    vmem = pl.BlockSpec(memory_space=pltpu.VMEM)
    own = own_keys.shape[0]
    return pl.pallas_call(
        prepare_kernel,
        out_shape=(
            pltpu.VMEM((HD, values.shape[0]), bf16),
            pltpu.VMEM((own, HD), bf16),
            pltpu.VMEM((HD, own), bf16),
            jax.ShapeDtypeStruct((1, 1), f32),
        ),
        out_specs=(vmem, vmem, vmem, pl.BlockSpec(memory_space=pltpu.SMEM)),
        compiler_params=pltpu.CompilerParams(vmem_limit_bytes=20 << 20),
        name="prepare",
    )(values, own_keys, own_values)


def replicate_kernel(x_ref, out_ref, sems):
    moves = [
        pltpu.make_async_copy(x_ref, out_ref.at[at], sems.at[at]) for at in range(out_ref.shape[0])
    ]
    for move in moves:
        move.start()
    for move in moves:
        move.wait()


def replicate(array, count):
    return pl.pallas_call(
        replicate_kernel,
        out_shape=jax.ShapeDtypeStruct((count,) + array.shape, array.dtype),
        in_specs=[pl.BlockSpec(memory_space=pltpu.HBM)],
        out_specs=pl.BlockSpec(memory_space=pl.ANY),
        scratch_shapes=[pltpu.SemaphoreType.DMA((count,))],
        compiler_params=pltpu.CompilerParams(vmem_limit_bytes=20 << 20),
        name="replicate",
    )(array)


def attend_kernel(
    lead, group, stack, key_block, q_ref, k_ref, vt_ref, rk_ref, rvt_ref, bias_ref, fact_ref, out_ref,
    logs_ref,
):
    tokens = q_ref.shape[0]
    keys = k_ref.shape[0]

    def scores(keys_block, q):
        return (
            lax.dot_general(
                keys_block, q, (((1,), (1,)), ((), ())), preferred_element_type=f32
            )
            * SCALE2
        )

    def product(columns, weights):
        return jnp.dot(columns, weights.astype(bf16), preferred_element_type=f32)

    def result_of(total, sums):
        return (total / sums).T.astype(bf16)

    def logs_rows(rows):
        pieces = split3(jnp.concatenate(rows, axis=0))
        out_ref[group * tokens :, :] = jnp.concatenate(
            pieces + (jnp.zeros((group, tokens), f32),), axis=0
        ).astype(bf16)

    def fold(weights):
        return jnp.sum(weights.reshape(-1, 8, weights.shape[1]), axis=0)

    everything, logs = [], []
    bias = jnp.concatenate([bias_ref[...]] * stack, axis=1)
    for first in range(0, group, stack):
        q = jnp.concatenate(
            [
                q_ref[:, head * HD : (head + 1) * HD]
                for head in range(lead + first, lead + first + stack)
            ],
            axis=0,
        )
        total, sums = None, None
        now = scores(k_ref[:key_block, :], q)
        for start in range(0, keys, key_block):
            later = start + key_block
            if later < keys:
                following = scores(k_ref[later : later + key_block, :], q)
            else:
                following = scores(rk_ref[...], q) + bias
            weights = jnp.exp2(now)
            term = product(vt_ref[:, start:later], weights)
            total = term if total is None else total + term
            sums = fold(weights) if sums is None else sums + fold(weights)
            now = following
        weights = jnp.exp2(now)
        total += product(rvt_ref[...], weights)
        sums = jnp.sum(sums + fold(weights), axis=0, keepdims=True)
        everything.append(sums)
        log = jnp.log2(sums)
        for at in range(stack):
            lanes = slice(at * tokens, (at + 1) * tokens)
            logs.append(log[:, lanes])
            head = first + at
            out_ref[head * tokens : (head + 1) * tokens, :] = result_of(
                total[:, lanes], sums[:, lanes]
            )
    logs_rows(logs)
    sums = jnp.concatenate(everything, axis=1)
    outside = jnp.where((sums >= LOWEST) & (sums <= HIGHEST), f32(0), f32(1))
    inside = (jnp.max(outside) < 0.5) & (fact_ref[0, 0] >= SMALL)

    @pl.when(jnp.logical_not(inside))
    def _():
        @pl.loop(0, group)
        def _(head):
            q = q_ref[:, pl.ds(pl.multiple_of((lead + head) * HD, HD), HD)]
            mine = scores(rk_ref[...], q) + bias_ref[...]
            rest = scores(k_ref[...], q)
            top = jnp.maximum(
                jnp.max(mine, axis=0, keepdims=True), jnp.max(rest, axis=0, keepdims=True)
            )
            mine, rest = jnp.exp2(mine - top), jnp.exp2(rest - top)
            total = product(rvt_ref[...], mine) + product(vt_ref[...], rest)
            sums = jnp.sum(mine, axis=0, keepdims=True) + jnp.sum(rest, axis=0, keepdims=True)
            logs_ref[pl.ds(head, 1), :] = jnp.log2(sums) + top
            out_ref[pl.ds(pl.multiple_of(head * tokens, tokens), tokens), :] = result_of(
                total, sums
            )

        logs_rows([logs_ref[...]])


def attend(lead, group, queries, keys, columns, own_keys, own_columns, bias, fact):
    tokens = queries.shape[0]
    vmem = pl.BlockSpec(memory_space=pltpu.VMEM)
    return pl.pallas_call(
        lambda *refs: attend_kernel(lead, group, min(4, group), 512, *refs),
        out_shape=jax.ShapeDtypeStruct((group * (tokens + DEPTH), HD), bf16),
        in_specs=[vmem] * 6 + [pl.BlockSpec(memory_space=pltpu.SMEM)],
        out_specs=vmem,
        scratch_shapes=[pltpu.VMEM((group, tokens), f32)],
        compiler_params=pltpu.CompilerParams(vmem_limit_bytes=20 << 20),
        name="attend",
    )(queries, keys, columns, own_keys, own_columns, bias, fact)


def join_kernel(group, halves, *refs):
    own_refs, part_refs, out_ref = refs[:halves], refs[halves:-1], refs[-1]
    owners = out_ref.shape[0]
    tokens = part_refs[0].shape[0] // group - DEPTH
    few = group // halves

    def log_of(ref, heads):
        pieces = ref[heads * tokens :, :].astype(f32)
        return sum(pieces[at * heads : (at + 1) * heads] for at in range(3))

    def part_of(at, head):
        ref = part_refs[at - 1] if at else own_refs[head // few]
        row = head * tokens if at else head % few * tokens
        return ref[row : row + tokens, :].astype(f32)

    logs = [jnp.concatenate([log_of(ref, few) for ref in own_refs], axis=0)]
    logs += [log_of(ref, group) for ref in part_refs]
    top = logs[0]
    for log in logs[1:]:
        top = jnp.maximum(top, log)
    shares = [jnp.exp2(log - top) for log in logs]
    whole = sum(shares)
    shares = [share / whole for share in shares]
    rows = list(split3(top + jnp.log2(whole))) + shares
    rows.append(jnp.zeros((HD - group * len(rows), tokens), f32))
    turned = jnp.concatenate(rows, axis=0).T
    split = tokens // owners
    for head in range(group):
        total = None
        for at in range(len(shares)):
            lane = (3 + at) * group + head
            term = part_of(at, head) * turned[:, lane : lane + 1]
            total = term if total is None else total + term
        out_ref[:, head * split : (head + 1) * split, :] = total.astype(bf16).reshape(
            owners, split, HD
        )
    out_ref[:, group * split :, :] = turned.astype(bf16).reshape(owners, split, HD)


def join(own, parts, group, owners):
    tokens = parts[0].shape[0] // group - DEPTH
    return pl.pallas_call(
        lambda *refs: join_kernel(group, len(own), *refs),
        out_shape=jax.ShapeDtypeStruct((owners, (group + 1) * (tokens // owners), HD), bf16),
        compiler_params=pltpu.CompilerParams(vmem_limit_bytes=20 << 20),
        name="join",
    )(*own, *parts)


def combine_kernel(group, parts_ref, out_ref):
    copies, tokens, _ = out_ref.shape
    pieces = parts_ref[:, group * tokens :, :].astype(f32)
    logs = sum(pieces[:, :, piece * group : (piece + 1) * group] for piece in range(3))
    share = jnp.exp2(logs - jnp.max(logs, axis=0, keepdims=True))
    share = share / jnp.sum(share, axis=0, keepdims=True)
    for head in range(group):
        part = parts_ref[:, head * tokens : (head + 1) * tokens, :].astype(f32)
        result = jnp.sum(part * share[:, :, head : head + 1], axis=0).astype(bf16)
        out_ref[:, :, head * HD : (head + 1) * HD] = jnp.broadcast_to(
            result[None], (copies, tokens, HD)
        )


def combine(parts, group):
    owners, height, _ = parts.shape
    return pl.pallas_call(
        lambda *refs: combine_kernel(group, *refs),
        out_shape=jax.ShapeDtypeStruct((owners, height // (group + 1), group * HD), bf16),
        compiler_params=pltpu.CompilerParams(vmem_limit_bytes=20 << 20),
        name="combine",
    )(parts)


Y, Z = 4, 8


def on_device(queries, prefix_keys, prefix_values, resp_keys, resp_values, segment_ids, out_weight):
    ways = lax.axis_size("mp")
    tokens, width = queries.shape
    group = width // HD
    rows = segment_ids.shape[0]
    quarter = rows // Y
    along_z = [[y * Z + z for z in range(Z)] for y in range(Y)]
    place = lax.axis_index("seq")

    def across_z(array):
        return lax.all_to_all(array, "seq", 0, 0, axis_index_groups=along_z, tiled=True)

    def along_y(array, step):
        pairs = [(y * Z + z, (y + step) % Y * Z + z) for y in range(Y) for z in range(Z)]
        return lax.ppermute(array, "seq", pairs)

    mine = across_z(replicate(queries, Z)).reshape(quarter, width)

    columns, own_keys, own_columns, fact = prepare(prefix_values, resp_keys, resp_values)
    first = place * tokens
    own_segments = lax.dynamic_slice_in_dim(segment_ids, first, tokens)
    own_rows = first + jnp.arange(tokens, dtype=jnp.int32)
    allowed = (own_segments[:, None] == segment_ids[None, :]) & (
        own_rows[:, None] <= jnp.arange(rows, dtype=jnp.int32)[None, :]
    )
    bias = jnp.where(allowed, f32(0), f32(-1e30))

    def bias_for(step):
        owner = (place // Z + Y - step) % Y
        return lax.dynamic_slice_in_dim(bias, owner * quarter, quarter, 1)

    def part_for(array, block, lead=0, count=group):
        return attend(
            lead, count, array, prefix_keys, columns, own_keys, own_columns, block, fact
        )

    blocks = [bias_for(step) for step in range(Y)]
    mine, columns, own_keys, own_columns, fact, *blocks = lax.optimization_barrier(
        (mine, columns, own_keys, own_columns, fact, *blocks)
    )
    arrivals = {step: along_y(mine, step) for step in (1, 3, 2)}
    own = [part_for(mine, blocks[0], 0, group // 2)]
    *blocks, own[0] = lax.optimization_barrier((*blocks, own[0]))
    parts = [along_y(part_for(arrivals[step], blocks[step]), -step) for step in (1, 2, 3)]
    own.append(part_for(mine, blocks[0], group // 2, group // 2))

    joined = across_z(join(own, parts, group, Z))
    heads = across_z(combine(joined, group)).reshape(quarter, width)
    pieces = [heads] + [along_y(heads, step) for step in (1, 3, 2)]
    scored = [
        jnp.dot(piece, out_weight, preferred_element_type=f32).astype(bf16) for piece in pieces
    ]
    order = (0, 1, 3, 2)
    whole = jnp.zeros((rows, out_weight.shape[1]), bf16)
    for step, piece in zip(order, scored):
        owner = (place // Z + Y - step) % Y
        whole = lax.dynamic_update_slice_in_dim(whole, piece, owner * quarter, 0)
    scored = whole.reshape(ways, rows // ways, -1)
    scored = lax.all_to_all(scored, "mp", 0, 0, tiled=True)
    return jnp.sum(scored.astype(f32), axis=0).astype(bf16)


def solution(mesh):
    in_specs = (
        P("seq", "mp"),
        P("seq", "mp"),
        P("seq", "mp"),
        P("seq", "mp"),
        P("seq", "mp"),
        P(),
        P("mp", "seq"),
    )
    return jax.shard_map(
        on_device, mesh=mesh, in_specs=in_specs, out_specs=P("mp", "seq"), check_vma=False
    )
```

```python
import jax
import jax.numpy as jnp
from jax import lax
from jax.experimental import pallas as pl
from jax.experimental.pallas import tpu as pltpu
from jax.sharding import PartitionSpec as P

HD = 128
SCALE2 = HD**-0.5 * 1.4426950408889634
LOWEST = 2.0**-60
HIGHEST = 2.0**100
SMALL = 2.0**-20
DEPTH = 4
f32 = jnp.float32
bf16 = jnp.bfloat16


def split3(x):
    high = x.astype(bf16).astype(f32)
    rest = x - high
    middle = rest.astype(bf16).astype(f32)
    return high, middle, rest - middle


def prepare_kernel(v_ref, rk_ref, rv_ref, vt_ref, rk_out_ref, rvt_ref, fact_ref):
    v, rv = v_ref[...], rv_ref[...]
    vt_ref[...] = v.T
    rk_out_ref[...] = rk_ref[...]
    rvt_ref[...] = rv.T
    fact_ref[0, 0] = jnp.maximum(
        jnp.max(jnp.abs(v.astype(f32))), jnp.max(jnp.abs(rv.astype(f32)))
    )


def prepare(values, own_keys, own_values):
    vmem = pl.BlockSpec(memory_space=pltpu.VMEM)
    own = own_keys.shape[0]
    return pl.pallas_call(
        prepare_kernel,
        out_shape=(
            pltpu.VMEM((HD, values.shape[0]), bf16),
            pltpu.VMEM((own, HD), bf16),
            pltpu.VMEM((HD, own), bf16),
            jax.ShapeDtypeStruct((1, 1), f32),
        ),
        out_specs=(vmem, vmem, vmem, pl.BlockSpec(memory_space=pltpu.SMEM)),
        compiler_params=pltpu.CompilerParams(vmem_limit_bytes=20 << 20),
        name="prepare",
    )(values, own_keys, own_values)


def replicate_kernel(x_ref, out_ref, sems):
    moves = [
        pltpu.make_async_copy(x_ref, out_ref.at[at], sems.at[at]) for at in range(out_ref.shape[0])
    ]
    for move in moves:
        move.start()
    for move in moves:
        move.wait()


def replicate(array, count):
    return pl.pallas_call(
        replicate_kernel,
        out_shape=jax.ShapeDtypeStruct((count,) + array.shape, array.dtype),
        in_specs=[pl.BlockSpec(memory_space=pltpu.HBM)],
        out_specs=pl.BlockSpec(memory_space=pl.ANY),
        scratch_shapes=[pltpu.SemaphoreType.DMA((count,))],
        compiler_params=pltpu.CompilerParams(vmem_limit_bytes=20 << 20),
        name="replicate",
    )(array)


def attend_kernel(
    lead, group, stack, key_block, q_ref, k_ref, vt_ref, rk_ref, rvt_ref, bias_ref, fact_ref, out_ref,
    logs_ref,
):
    tokens = q_ref.shape[0]
    keys = k_ref.shape[0]

    def scores(keys_block, q):
        return (
            lax.dot_general(
                keys_block, q, (((1,), (1,)), ((), ())), preferred_element_type=f32
            )
            * SCALE2
        )

    def product(columns, weights):
        return jnp.dot(columns, weights.astype(bf16), preferred_element_type=f32)

    def result_of(total, sums):
        return (total / sums).T.astype(bf16)

    def logs_rows(rows):
        pieces = split3(jnp.concatenate(rows, axis=0))
        out_ref[group * tokens :, :] = jnp.concatenate(
            pieces + (jnp.zeros((group, tokens), f32),), axis=0
        ).astype(bf16)

    def fold(weights):
        return jnp.sum(weights.reshape(-1, 8, weights.shape[1]), axis=0)

    everything, logs = [], []
    bias = jnp.concatenate([bias_ref[...]] * stack, axis=1)
    for first in range(0, group, stack):
        q = jnp.concatenate(
            [
                q_ref[:, head * HD : (head + 1) * HD]
                for head in range(lead + first, lead + first + stack)
            ],
            axis=0,
        )
        total, sums = None, None
        now = scores(k_ref[:key_block, :], q)
        for start in range(0, keys, key_block):
            later = start + key_block
            if later < keys:
                following = scores(k_ref[later : later + key_block, :], q)
            else:
                following = scores(rk_ref[...], q) + bias
            weights = jnp.exp2(now)
            term = product(vt_ref[:, start:later], weights)
            total = term if total is None else total + term
            sums = fold(weights) if sums is None else sums + fold(weights)
            now = following
        weights = jnp.exp2(now)
        total += product(rvt_ref[...], weights)
        sums = jnp.sum(sums + fold(weights), axis=0, keepdims=True)
        everything.append(sums)
        log = jnp.log2(sums)
        for at in range(stack):
            lanes = slice(at * tokens, (at + 1) * tokens)
            logs.append(log[:, lanes])
            head = first + at
            out_ref[head * tokens : (head + 1) * tokens, :] = result_of(
                total[:, lanes], sums[:, lanes]
            )
    logs_rows(logs)
    sums = jnp.concatenate(everything, axis=1)
    outside = jnp.where((sums >= LOWEST) & (sums <= HIGHEST), f32(0), f32(1))
    inside = (jnp.max(outside) < 0.5) & (fact_ref[0, 0] >= SMALL)

    @pl.when(jnp.logical_not(inside))
    def _():
        @pl.loop(0, group)
        def _(head):
            q = q_ref[:, pl.ds(pl.multiple_of((lead + head) * HD, HD), HD)]
            mine = scores(rk_ref[...], q) + bias_ref[...]
            rest = scores(k_ref[...], q)
            top = jnp.maximum(
                jnp.max(mine, axis=0, keepdims=True), jnp.max(rest, axis=0, keepdims=True)
            )
            mine, rest = jnp.exp2(mine - top), jnp.exp2(rest - top)
            total = product(rvt_ref[...], mine) + product(vt_ref[...], rest)
            sums = jnp.sum(mine, axis=0, keepdims=True) + jnp.sum(rest, axis=0, keepdims=True)
            logs_ref[pl.ds(head, 1), :] = jnp.log2(sums) + top
            out_ref[pl.ds(pl.multiple_of(head * tokens, tokens), tokens), :] = result_of(
                total, sums
            )

        logs_rows([logs_ref[...]])


def attend(lead, group, queries, keys, columns, own_keys, own_columns, bias, fact):
    tokens = queries.shape[0]
    vmem = pl.BlockSpec(memory_space=pltpu.VMEM)
    return pl.pallas_call(
        lambda *refs: attend_kernel(lead, group, min(4, group), 512, *refs),
        out_shape=jax.ShapeDtypeStruct((group * (tokens + DEPTH), HD), bf16),
        in_specs=[vmem] * 6 + [pl.BlockSpec(memory_space=pltpu.SMEM)],
        out_specs=vmem,
        scratch_shapes=[pltpu.VMEM((group, tokens), f32)],
        compiler_params=pltpu.CompilerParams(vmem_limit_bytes=20 << 20),
        name="attend",
    )(queries, keys, columns, own_keys, own_columns, bias, fact)


def join_kernel(group, halves, *refs):
    own_refs, part_refs, out_ref = refs[:halves], refs[halves:-1], refs[-1]
    owners = out_ref.shape[0]
    tokens = part_refs[0].shape[0] // group - DEPTH
    few = group // halves

    def log_of(ref, heads):
        pieces = ref[heads * tokens :, :].astype(f32)
        return sum(pieces[at * heads : (at + 1) * heads] for at in range(3))

    def part_of(at, head):
        ref = part_refs[at - 1] if at else own_refs[head // few]
        row = head * tokens if at else head % few * tokens
        return ref[row : row + tokens, :].astype(f32)

    logs = [jnp.concatenate([log_of(ref, few) for ref in own_refs], axis=0)]
    logs += [log_of(ref, group) for ref in part_refs]
    top = logs[0]
    for log in logs[1:]:
        top = jnp.maximum(top, log)
    shares = [jnp.exp2(log - top) for log in logs]
    whole = sum(shares)
    shares = [share / whole for share in shares]
    rows = list(split3(top + jnp.log2(whole))) + shares
    rows.append(jnp.zeros((HD - group * len(rows), tokens), f32))
    turned = jnp.concatenate(rows, axis=0).T
    split = tokens // owners
    for head in range(group):
        total = None
        for at in range(len(shares)):
            lane = (3 + at) * group + head
            term = part_of(at, head) * turned[:, lane : lane + 1]
            total = term if total is None else total + term
        out_ref[:, head * split : (head + 1) * split, :] = total.astype(bf16).reshape(
            owners, split, HD
        )
    out_ref[:, group * split :, :] = turned.astype(bf16).reshape(owners, split, HD)


def join(own, parts, group, owners):
    tokens = parts[0].shape[0] // group - DEPTH
    return pl.pallas_call(
        lambda *refs: join_kernel(group, len(own), *refs),
        out_shape=jax.ShapeDtypeStruct((owners, (group + 1) * (tokens // owners), HD), bf16),
        compiler_params=pltpu.CompilerParams(vmem_limit_bytes=20 << 20),
        name="join",
    )(*own, *parts)


def combine_kernel(group, parts_ref, out_ref):
    copies, tokens, _ = out_ref.shape
    pieces = parts_ref[:, group * tokens :, :].astype(f32)
    logs = sum(pieces[:, :, piece * group : (piece + 1) * group] for piece in range(3))
    share = jnp.exp2(logs - jnp.max(logs, axis=0, keepdims=True))
    share = share / jnp.sum(share, axis=0, keepdims=True)
    for head in range(group):
        part = parts_ref[:, head * tokens : (head + 1) * tokens, :].astype(f32)
        result = jnp.sum(part * share[:, :, head : head + 1], axis=0).astype(bf16)
        out_ref[:, :, head * HD : (head + 1) * HD] = jnp.broadcast_to(
            result[None], (copies, tokens, HD)
        )


def combine(parts, group):
    owners, height, _ = parts.shape
    return pl.pallas_call(
        lambda *refs: combine_kernel(group, *refs),
        out_shape=jax.ShapeDtypeStruct((owners, height // (group + 1), group * HD), bf16),
        compiler_params=pltpu.CompilerParams(vmem_limit_bytes=20 << 20),
        name="combine",
    )(parts)


Y, Z = 4, 8


def on_device(queries, prefix_keys, prefix_values, resp_keys, resp_values, segment_ids, out_weight):
    ways = lax.axis_size("mp")
    tokens, width = queries.shape
    group = width // HD
    rows = segment_ids.shape[0]
    quarter = rows // Y
    along_z = [[y * Z + z for z in range(Z)] for y in range(Y)]
    place = lax.axis_index("seq")

    def across_z(array):
        return lax.all_to_all(array, "seq", 0, 0, axis_index_groups=along_z, tiled=True)

    def along_y(array, step):
        pairs = [(y * Z + z, (y + step) % Y * Z + z) for y in range(Y) for z in range(Z)]
        return lax.ppermute(array, "seq", pairs)

    mine = across_z(replicate(queries, Z)).reshape(quarter, width)

    columns, own_keys, own_columns, fact = prepare(prefix_values, resp_keys, resp_values)
    first = place * tokens
    own_segments = lax.dynamic_slice_in_dim(segment_ids, first, tokens)
    own_rows = first + jnp.arange(tokens, dtype=jnp.int32)
    allowed = (own_segments[:, None] == segment_ids[None, :]) & (
        own_rows[:, None] <= jnp.arange(rows, dtype=jnp.int32)[None, :]
    )
    bias = jnp.where(allowed, f32(0), f32(-1e30))

    def bias_for(step):
        owner = (place // Z + Y - step) % Y
        return lax.dynamic_slice_in_dim(bias, owner * quarter, quarter, 1)

    def part_for(array, block, lead=0, count=group):
        return attend(
            lead, count, array, prefix_keys, columns, own_keys, own_columns, block, fact
        )

    blocks = [bias_for(step) for step in range(Y)]
    mine, columns, own_keys, own_columns, fact, *blocks = lax.optimization_barrier(
        (mine, columns, own_keys, own_columns, fact, *blocks)
    )
    arrivals = {step: along_y(mine, step) for step in (1, 3)}
    own = [part_for(mine, blocks[0], 0, group // 2)]
    *blocks, later, own[0] = lax.optimization_barrier((*blocks, mine, own[0]))
    arrivals[2] = along_y(later, 2)
    parts = [along_y(part_for(arrivals[step], blocks[step]), -step) for step in (1, 2, 3)]
    own.append(part_for(mine, blocks[0], group // 2, group // 2))

    joined = across_z(join(own, parts, group, Z))
    heads = across_z(combine(joined, group)).reshape(quarter, width)
    pieces = [heads] + [along_y(heads, step) for step in (1, 3, 2)]
    scored = [
        jnp.dot(piece, out_weight, preferred_element_type=f32).astype(bf16) for piece in pieces
    ]
    order = (0, 1, 3, 2)
    whole = jnp.zeros((rows, out_weight.shape[1]), bf16)
    for step, piece in zip(order, scored):
        owner = (place // Z + Y - step) % Y
        whole = lax.dynamic_update_slice_in_dim(whole, piece, owner * quarter, 0)
    scored = whole.reshape(ways, rows // ways, -1)
    scored = lax.all_to_all(scored, "mp", 0, 0, tiled=True)
    return jnp.sum(scored.astype(f32), axis=0).astype(bf16)


def solution(mesh):
    in_specs = (
        P("seq", "mp"),
        P("seq", "mp"),
        P("seq", "mp"),
        P("seq", "mp"),
        P("seq", "mp"),
        P(),
        P("mp", "seq"),
    )
    return jax.shard_map(
        on_device, mesh=mesh, in_specs=in_specs, out_specs=P("mp", "seq"), check_vma=False
    )
```

```python
import jax
import jax.numpy as jnp
from jax import lax
from jax.experimental import pallas as pl
from jax.experimental.pallas import tpu as pltpu
from jax.sharding import PartitionSpec as P

HD = 128
SCALE2 = HD**-0.5 * 1.4426950408889634
LOWEST = 2.0**-60
HIGHEST = 2.0**100
SMALL = 2.0**-20
DEPTH = 4
f32 = jnp.float32
bf16 = jnp.bfloat16


def split3(x):
    high = x.astype(bf16).astype(f32)
    rest = x - high
    middle = rest.astype(bf16).astype(f32)
    return high, middle, rest - middle


def prepare_kernel(v_ref, rk_ref, rv_ref, vt_ref, rk_out_ref, rvt_ref, fact_ref):
    v, rv = v_ref[...], rv_ref[...]
    vt_ref[...] = v.T
    rk_out_ref[...] = rk_ref[...]
    rvt_ref[...] = rv.T
    fact_ref[0, 0] = jnp.maximum(
        jnp.max(jnp.abs(v.astype(f32))), jnp.max(jnp.abs(rv.astype(f32)))
    )


def prepare(values, own_keys, own_values):
    vmem = pl.BlockSpec(memory_space=pltpu.VMEM)
    own = own_keys.shape[0]
    return pl.pallas_call(
        prepare_kernel,
        out_shape=(
            pltpu.VMEM((HD, values.shape[0]), bf16),
            pltpu.VMEM((own, HD), bf16),
            pltpu.VMEM((HD, own), bf16),
            jax.ShapeDtypeStruct((1, 1), f32),
        ),
        out_specs=(vmem, vmem, vmem, pl.BlockSpec(memory_space=pltpu.SMEM)),
        compiler_params=pltpu.CompilerParams(vmem_limit_bytes=20 << 20),
        name="prepare",
    )(values, own_keys, own_values)


def replicate_kernel(x_ref, out_ref, sems):
    moves = [
        pltpu.make_async_copy(x_ref, out_ref.at[at], sems.at[at]) for at in range(out_ref.shape[0])
    ]
    for move in moves:
        move.start()
    for move in moves:
        move.wait()


def replicate(array, count):
    return pl.pallas_call(
        replicate_kernel,
        out_shape=jax.ShapeDtypeStruct((count,) + array.shape, array.dtype),
        in_specs=[pl.BlockSpec(memory_space=pltpu.HBM)],
        out_specs=pl.BlockSpec(memory_space=pl.ANY),
        scratch_shapes=[pltpu.SemaphoreType.DMA((count,))],
        compiler_params=pltpu.CompilerParams(vmem_limit_bytes=20 << 20),
        name="replicate",
    )(array)


def attend_kernel(
    lead, group, stack, key_block, q_ref, k_ref, vt_ref, rk_ref, rvt_ref, bias_ref, fact_ref, out_ref,
    logs_ref,
):
    tokens = q_ref.shape[0]
    keys = k_ref.shape[0]

    def scores(keys_block, q):
        return (
            lax.dot_general(
                keys_block, q, (((1,), (1,)), ((), ())), preferred_element_type=f32
            )
            * SCALE2
        )

    def product(columns, weights):
        return jnp.dot(columns, weights.astype(bf16), preferred_element_type=f32)

    def result_of(total, sums):
        return (total / sums).T.astype(bf16)

    def logs_rows(rows):
        pieces = split3(jnp.concatenate(rows, axis=0))
        out_ref[group * tokens :, :] = jnp.concatenate(
            pieces + (jnp.zeros((group, tokens), f32),), axis=0
        ).astype(bf16)

    def fold(weights):
        return jnp.sum(weights.reshape(-1, 8, weights.shape[1]), axis=0)

    everything, logs = [], []
    bias = jnp.concatenate([bias_ref[...]] * stack, axis=1)
    for first in range(0, group, stack):
        q = jnp.concatenate(
            [
                q_ref[:, head * HD : (head + 1) * HD]
                for head in range(lead + first, lead + first + stack)
            ],
            axis=0,
        )
        total, sums = None, None
        now = scores(k_ref[:key_block, :], q)
        for start in range(0, keys, key_block):
            later = start + key_block
            if later < keys:
                following = scores(k_ref[later : later + key_block, :], q)
            else:
                following = scores(rk_ref[...], q) + bias
            weights = jnp.exp2(now)
            term = product(vt_ref[:, start:later], weights)
            total = term if total is None else total + term
            sums = fold(weights) if sums is None else sums + fold(weights)
            now = following
        weights = jnp.exp2(now)
        total += product(rvt_ref[...], weights)
        sums = jnp.sum(sums + fold(weights), axis=0, keepdims=True)
        everything.append(sums)
        log = jnp.log2(sums)
        for at in range(stack):
            lanes = slice(at * tokens, (at + 1) * tokens)
            logs.append(log[:, lanes])
            head = first + at
            out_ref[head * tokens : (head + 1) * tokens, :] = result_of(
                total[:, lanes], sums[:, lanes]
            )
    logs_rows(logs)
    sums = jnp.concatenate(everything, axis=1)
    outside = jnp.where((sums >= LOWEST) & (sums <= HIGHEST), f32(0), f32(1))
    inside = (jnp.max(outside) < 0.5) & (fact_ref[0, 0] >= SMALL)

    @pl.when(jnp.logical_not(inside))
    def _():
        @pl.loop(0, group)
        def _(head):
            q = q_ref[:, pl.ds(pl.multiple_of((lead + head) * HD, HD), HD)]
            mine = scores(rk_ref[...], q) + bias_ref[...]
            rest = scores(k_ref[...], q)
            top = jnp.maximum(
                jnp.max(mine, axis=0, keepdims=True), jnp.max(rest, axis=0, keepdims=True)
            )
            mine, rest = jnp.exp2(mine - top), jnp.exp2(rest - top)
            total = product(rvt_ref[...], mine) + product(vt_ref[...], rest)
            sums = jnp.sum(mine, axis=0, keepdims=True) + jnp.sum(rest, axis=0, keepdims=True)
            logs_ref[pl.ds(head, 1), :] = jnp.log2(sums) + top
            out_ref[pl.ds(pl.multiple_of(head * tokens, tokens), tokens), :] = result_of(
                total, sums
            )

        logs_rows([logs_ref[...]])


def attend(lead, group, queries, keys, columns, own_keys, own_columns, bias, fact):
    tokens = queries.shape[0]
    vmem = pl.BlockSpec(memory_space=pltpu.VMEM)
    return pl.pallas_call(
        lambda *refs: attend_kernel(lead, group, min(4, group), 512, *refs),
        out_shape=jax.ShapeDtypeStruct((group * (tokens + DEPTH), HD), bf16),
        in_specs=[vmem] * 6 + [pl.BlockSpec(memory_space=pltpu.SMEM)],
        out_specs=vmem,
        scratch_shapes=[pltpu.VMEM((group, tokens), f32)],
        compiler_params=pltpu.CompilerParams(vmem_limit_bytes=20 << 20),
        name="attend",
    )(queries, keys, columns, own_keys, own_columns, bias, fact)


def join_kernel(group, halves, *refs):
    own_refs, part_refs, out_ref = refs[:halves], refs[halves:-1], refs[-1]
    owners = out_ref.shape[0]
    tokens = part_refs[0].shape[0] // group - DEPTH
    few = group // halves

    def log_of(ref, heads):
        pieces = ref[heads * tokens :, :].astype(f32)
        return sum(pieces[at * heads : (at + 1) * heads] for at in range(3))

    def part_of(at, head):
        ref = part_refs[at - 1] if at else own_refs[head // few]
        row = head * tokens if at else head % few * tokens
        return ref[row : row + tokens, :].astype(f32)

    logs = [jnp.concatenate([log_of(ref, few) for ref in own_refs], axis=0)]
    logs += [log_of(ref, group) for ref in part_refs]
    top = logs[0]
    for log in logs[1:]:
        top = jnp.maximum(top, log)
    shares = [jnp.exp2(log - top) for log in logs]
    whole = sum(shares)
    shares = [share / whole for share in shares]
    rows = list(split3(top + jnp.log2(whole))) + shares
    rows.append(jnp.zeros((HD - group * len(rows), tokens), f32))
    turned = jnp.concatenate(rows, axis=0).T
    split = tokens // owners
    for head in range(group):
        total = None
        for at in range(len(shares)):
            lane = (3 + at) * group + head
            term = part_of(at, head) * turned[:, lane : lane + 1]
            total = term if total is None else total + term
        out_ref[:, head * split : (head + 1) * split, :] = total.astype(bf16).reshape(
            owners, split, HD
        )
    out_ref[:, group * split :, :] = turned.astype(bf16).reshape(owners, split, HD)


def join(own, parts, group, owners):
    tokens = parts[0].shape[0] // group - DEPTH
    return pl.pallas_call(
        lambda *refs: join_kernel(group, len(own), *refs),
        out_shape=jax.ShapeDtypeStruct((owners, (group + 1) * (tokens // owners), HD), bf16),
        compiler_params=pltpu.CompilerParams(vmem_limit_bytes=20 << 20),
        name="join",
    )(*own, *parts)


def combine_kernel(group, parts_ref, out_ref):
    copies, tokens, _ = out_ref.shape
    pieces = parts_ref[:, group * tokens :, :].astype(f32)
    logs = sum(pieces[:, :, piece * group : (piece + 1) * group] for piece in range(3))
    share = jnp.exp2(logs - jnp.max(logs, axis=0, keepdims=True))
    share = share / jnp.sum(share, axis=0, keepdims=True)
    for head in range(group):
        part = parts_ref[:, head * tokens : (head + 1) * tokens, :].astype(f32)
        result = jnp.sum(part * share[:, :, head : head + 1], axis=0).astype(bf16)
        out_ref[:, :, head * HD : (head + 1) * HD] = jnp.broadcast_to(
            result[None], (copies, tokens, HD)
        )


def combine(parts, group):
    owners, height, _ = parts.shape
    return pl.pallas_call(
        lambda *refs: combine_kernel(group, *refs),
        out_shape=jax.ShapeDtypeStruct((owners, height // (group + 1), group * HD), bf16),
        compiler_params=pltpu.CompilerParams(vmem_limit_bytes=20 << 20),
        name="combine",
    )(parts)


Y, Z = 4, 8


def on_device(queries, prefix_keys, prefix_values, resp_keys, resp_values, segment_ids, out_weight):
    ways = lax.axis_size("mp")
    tokens, width = queries.shape
    group = width // HD
    rows = segment_ids.shape[0]
    quarter = rows // Y
    along_z = [[y * Z + z for z in range(Z)] for y in range(Y)]
    place = lax.axis_index("seq")

    def across_z(array):
        return lax.all_to_all(array, "seq", 0, 0, axis_index_groups=along_z, tiled=True)

    def along_y(array, step):
        pairs = [(y * Z + z, (y + step) % Y * Z + z) for y in range(Y) for z in range(Z)]
        return lax.ppermute(array, "seq", pairs)

    mine = across_z(replicate(queries, Z)).reshape(quarter, width)

    columns, own_keys, own_columns, fact = prepare(prefix_values, resp_keys, resp_values)
    first = place * tokens
    own_segments = lax.dynamic_slice_in_dim(segment_ids, first, tokens)
    own_rows = first + jnp.arange(tokens, dtype=jnp.int32)
    allowed = (own_segments[:, None] == segment_ids[None, :]) & (
        own_rows[:, None] <= jnp.arange(rows, dtype=jnp.int32)[None, :]
    )
    bias = jnp.where(allowed, f32(0), f32(-1e30))

    def bias_for(step):
        owner = (place // Z + Y - step) % Y
        return lax.dynamic_slice_in_dim(bias, owner * quarter, quarter, 1)

    def part_for(array, block, lead=0, count=group):
        return attend(
            lead, count, array, prefix_keys, columns, own_keys, own_columns, block, fact
        )

    blocks = [bias_for(step) for step in range(Y)]
    mine, columns, own_keys, own_columns, fact, *blocks = lax.optimization_barrier(
        (mine, columns, own_keys, own_columns, fact, *blocks)
    )
    arrivals = {step: along_y(mine, step) for step in (1, 3)}
    own = [part_for(mine, blocks[0], 0, group // 2)]
    *blocks, later, own[0] = lax.optimization_barrier((*blocks, mine, own[0]))
    arrivals[2] = along_y(later, 2)
    parts = [along_y(part_for(arrivals[step], blocks[step]), -step) for step in (1, 2, 3)]
    own.append(part_for(mine, blocks[0], group // 2, group // 2))

    joined = across_z(join(own, parts, group, Z))
    heads = across_z(combine(joined, group)).reshape(quarter, width)
    pieces = [heads] + [along_y(heads, step) for step in (2, 1, 3)]
    scored = [
        jnp.dot(piece, out_weight, preferred_element_type=f32).astype(bf16) for piece in pieces
    ]
    order = (0, 2, 1, 3)
    whole = jnp.zeros((rows, out_weight.shape[1]), bf16)
    for step, piece in zip(order, scored):
        owner = (place // Z + Y - step) % Y
        whole = lax.dynamic_update_slice_in_dim(whole, piece, owner * quarter, 0)
    scored = whole.reshape(ways, rows // ways, -1)
    scored = lax.all_to_all(scored, "mp", 0, 0, tiled=True)
    return jnp.sum(scored.astype(f32), axis=0).astype(bf16)


def solution(mesh):
    in_specs = (
        P("seq", "mp"),
        P("seq", "mp"),
        P("seq", "mp"),
        P("seq", "mp"),
        P("seq", "mp"),
        P(),
        P("mp", "seq"),
    )
    return jax.shard_map(
        on_device, mesh=mesh, in_specs=in_specs, out_specs=P("mp", "seq"), check_vma=False
    )
```
